32 devices in a mesh: wide: 8 (over y, x, core), narrow: 4 (over z).
Axes of the slice: x: 2, y: 2, z: 4, core: 2. Of those that a mesh axis runs over, the one named last changes fastest.
Arguments:
- hidden: bfloat16 [2048, 2048], P(('wide', 'narrow')), may hold values from -6 to 6
- cotangent: bfloat16 [2048, 2048], P(('wide', 'narrow')), may hold values from -6 to 6
- routes: int32 [2048, 6], P(('wide', 'narrow')), may hold values from 0 to 15, all different within a row; in each aligned block of 64 rows (0 to 63, 64 to 127, ...) at most 48 rows name the same one
- gates: float32 [2048, 6], P(('wide', 'narrow')), may hold values from 0.05 to 1
- offsets: int32 [8], replicated, may hold values from 0 to 7, each once
- w_gate: bfloat16 [32, 2048, 704], P(('wide', 'narrow')), may hold values from -0.125 to 0.125
- w_up: bfloat16 [32, 2048, 704], P(('wide', 'narrow')), may hold values from -0.125 to 0.125
- w_down: bfloat16 [32, 704, 2048], P(('wide', 'narrow')), may hold values from -0.15625 to 0.15625
- w_out: bfloat16 [2048, 2048], P('narrow'), may hold values from -0.125 to 0.125
- latent: bfloat16 [2048, 512], P('wide'), may hold values from -6 to 6
- rope_key: bfloat16 [2048, 64], P('wide'), may hold values from -4 to 4
- q_nope: bfloat16 [2048, 2048], P('wide', 'narrow'), may hold values from -24 to 24
- q_pe: bfloat16 [2048, 1024], P('wide', 'narrow'), may hold values from -100 to 100
- w_uk: bfloat16 [2048, 512], P('narrow'), may hold values from -0.5 to 0.5
- w_uv: bfloat16 [2048, 512], P('narrow'), may hold values from -0.5 to 0.5
Outputs:
- resid_grad: bfloat16 [2048, 2048], P(('wide', 'narrow'))
- grad_q_nope: bfloat16 [2048, 2048], P('wide', 'narrow')
- grad_q_pe: bfloat16 [2048, 1024], P('wide', 'narrow')
- grad_latent: float32 [2048, 512], P(('wide', 'narrow'))
- grad_rope_key: float32 [2048, 64], P(('wide', 'narrow'))
The draws below stay inside these ranges and needn't reach their ends.
Inputs may be any that keep to these rules, and one draw needn't show every extreme that they name: `routes`: each row names 6 different experts; in each aligned block of 64 rows no expert is named by more than 48 rows, and in some blocks one is named by exactly 48. A permutation of the sequence blocks: token i of block b stands at position offsets[b] * 256 + i.
All inputs are finite; a program needn't handle non-finite values.
Results may differ from the reference program's by a relative error of at most 0.028.
Values may be sent and summed in bfloat16 or wider, within the bound.
No kernel may reach another device: no remote copies, remote signals or barrier semaphores. Data moves between devices by JAX's collectives and lax.ppermute only.
A program may use at most 128 MiB of HBM per device.

```python
import math
from functools import partial
import jax
import jax.numpy as jnp
import numpy as np
from jax import lax

D = 2048
FFE = 1408
TOPK = 6
HEADS = 16
LATENT = 512
NOPE = 128
ROPE = 64
VDIM = 128
TOK_WIDE = 256
TOKENS = 2048
TOK_DEV = 64
EXPERTS = 16
CAP = 48
N_WIDE = 8


def attention_plan(key):
    base = jax.random.fold_in(key, 9001)
    keys = jax.random.split(base, 8)
    rope = jnp.clip(jax.random.normal(keys[3], (TOKENS, ROPE)), -4.0, 4.0)
    return (rope, keys)


def draw_rope_key(key, part):
    rope, keys = attention_plan(key)
    return rope.astype(jnp.bfloat16)


def draw_q_pe(key, part):
    rope, keys = attention_plan(key)
    drawn = jnp.clip(jax.random.normal(keys[6], (TOKENS, HEADS, ROPE)), -4.0, 4.0)
    values = drawn
    return values.reshape(TOKENS, HEADS * ROPE).astype(jnp.bfloat16)


def draw_q_nope(key, part):
    rope, keys = attention_plan(key)
    values = jnp.clip(jax.random.normal(keys[7], (TOKENS, HEADS, NOPE)), -4.0, 4.0)
    return values.reshape(TOKENS, HEADS * NOPE).astype(jnp.bfloat16)


def level_of(stream_key, shape, cuts, least, high):
    level = 1.0
    for dim, blocks in cuts:
        heights = jax.random.uniform(jax.random.fold_in(jax.random.fold_in(stream_key, 6), dim), (blocks,), jnp.float32, least / len(cuts), high / len(cuts))
        level = level * jnp.repeat(jnp.exp(heights), shape[dim] // blocks).reshape((-1,) + (1,) * (len(shape) - 1 - dim))
    return level


def routed_block(stream_key, own, number, rows, number_of, top, limit, skew):
    order = jax.random.permutation(stream_key, number_of)
    crowded, common = shares(number_of, rows * top, limit, skew, True), shares(number_of, rows * top, limit, skew, False)
    places = jnp.arange(number_of)

    def named(tallies, rotation):
        used = int((tallies > 0).sum())
        fixed = max(1, used // 4)
        moved = fixed + (places - fixed + rotation * (used - fixed)) % max(1, number_of - fixed)
        return jnp.zeros((number_of,), jnp.int32).at[order[jnp.where(places < fixed, places, moved)]].set(jnp.asarray(tallies, jnp.int32))

    tallies = jnp.where(number % 4 == 0, named(crowded, number // 4), named(common, number - number // 4 - 1))
    mixed = jax.random.permutation(jax.random.fold_in(own, 3), number_of)
    giver, receiver = mixed[0:number_of // 2 * 2:2], mixed[1:number_of // 2 * 2:2]
    margin = jnp.minimum(tallies[giver] - 1, limit - tallies[receiver]) // 2
    margin = jnp.where((giver == order[0]) | (receiver == order[0]) | (tallies[receiver] == 0), 0, jnp.maximum(margin, 0))
    moved = jax.random.randint(jax.random.fold_in(own, 4), (number_of // 2,), 0, 1 << 20) % (margin + 1)
    tallies = tallies.at[giver].add(-moved).at[receiver].add(moved)
    items = jnp.searchsorted(jnp.cumsum(tallies), jnp.arange(rows * top), side="right").astype(jnp.int32)
    listing = items.reshape(top, rows).T
    listing = listing[jax.random.permutation(jax.random.fold_in(own, 1), rows)]
    rotation = jax.random.randint(jax.random.fold_in(own, 2), (rows, 1), 0, top)
    return jnp.take_along_axis(listing, (jnp.arange(top)[None, :] + rotation) % top, axis=1)


def shares(number_of, total, reach, lean, full):
    portions = [(1 << 20) // math.isqrt(rank ** lean) + 1 for rank in range(1, number_of + 1)]
    largest = reach if full else min(reach, max(-(-total // number_of), total * portions[0] // sum(portions)))
    least = 1 if total - largest >= number_of - 1 else 0
    holding, rest = [largest] + [least] * (number_of - 1), total - largest - least * (number_of - 1)
    while rest > 0:
        candidates = [i for i in range(1, number_of) if holding[i] < largest] or [i for i in range(1, number_of) if holding[i] < reach]
        mass, left = sum([portions[i] for i in candidates]), rest
        for i in candidates:
            addition = min(reach - holding[i], max(1, left * portions[i] // mass), rest)
            holding[i] = holding[i] + addition
            rest = rest - addition
    return np.array(holding)


def normal_values(stream_key, extent, width, reach, cuts=(), kind=jnp.bfloat16):
    factor_of = level_of(stream_key, extent, cuts, -0.22, 0.18) if cuts else 1.0
    result = jax.random.normal(stream_key, extent, jnp.float32) * width * factor_of
    return jnp.minimum(jnp.maximum(result, -reach), reach).astype(kind)


def setup_inputs(seed: int = 0) -> dict:
    key_of = jax.random.split(jax.random.key(seed), 16)
    hidden = normal_values(key_of[0], (TOKENS, D), 1.0, 6.0, ((0, 32),))
    cotangent = normal_values(key_of[1], (TOKENS, D), 1.0, 6.0, ((0, 32),))
    routes_keys = jax.random.split(jax.random.fold_in(key_of[2], 1), TOKENS // TOK_DEV)
    routes_turns = jax.random.permutation(jax.random.fold_in(key_of[2], 3), TOKENS // TOK_DEV)
    routes = jax.vmap(lambda own, number: routed_block(jax.random.fold_in(key_of[2], 2), own, number, TOK_DEV, EXPERTS, TOPK, CAP, 2))(routes_keys, routes_turns).reshape((TOKENS, TOPK))
    gates = jnp.clip(jnp.exp(math.log(1.0) - 2.9957323 * jax.random.uniform(key_of[3], (TOKENS, TOPK), jnp.float32) ** level_of(key_of[3], (TOKENS, TOPK), ((0, 32),), -0.2, 0.2)), 0.05, 1.0)
    offsets = jax.random.permutation(key_of[4], N_WIDE).astype(jnp.int32)
    w_gate = normal_values(key_of[5], (2 * EXPERTS, D, FFE // 2), D ** -0.5, 0.125, ((0, 32),))
    w_up = normal_values(key_of[6], (2 * EXPERTS, D, FFE // 2), D ** -0.5, 0.125, ((0, 32),))
    w_down = normal_values(key_of[7], (2 * EXPERTS, FFE // 2, D), FFE ** -0.5, 0.15625, ((0, 32),))
    w_out = normal_values(key_of[8], (HEADS * VDIM, D), D ** -0.5, 0.125, ((0, 4),))
    latent = normal_values(key_of[9], (TOKENS, LATENT), 1.0, 6.0, ((0, 8),))
    rope_key = draw_rope_key(jax.random.fold_in(key_of[15], 71), 0)
    q_nope = draw_q_nope(jax.random.fold_in(key_of[15], 71), 0)
    q_pe = draw_q_pe(jax.random.fold_in(key_of[15], 71), 0)
    w_uk = normal_values(key_of[13], (HEADS * NOPE, LATENT), NOPE ** -0.5, 0.5, ((0, 4),))
    w_uv = normal_values(key_of[14], (HEADS * VDIM, LATENT), VDIM ** -0.5, 0.5, ((0, 4),))
    return {"hidden": hidden, "cotangent": cotangent, "routes": routes, "gates": gates, "offsets": offsets, "w_gate": w_gate, "w_up": w_up, "w_down": w_down, "w_out": w_out, "latent": latent, "rope_key": rope_key, "q_nope": q_nope, "q_pe": q_pe, "w_uk": w_uk, "w_uv": w_uv}


def slot_numbers(expert_ids, experts):
    onehot = (expert_ids[:, None] == jnp.arange(experts, dtype=jnp.int32)[None, :]).astype(jnp.int32)
    before = jnp.cumsum(onehot, axis=0) - onehot
    return lax.optimization_barrier(jnp.sum(before * onehot, axis=1)).astype(jnp.int32)

def expert_grad(inputs):
    x_rows, dy_rows, gate_pair, up_pair, down_pair = inputs
    gate_full = jnp.concatenate([gate_pair[0], gate_pair[1]], axis=1)
    up_full = jnp.concatenate([up_pair[0], up_pair[1]], axis=1)
    down_full = jnp.concatenate([down_pair[0], down_pair[1]], axis=0)
    pre_gate = jnp.dot(x_rows, gate_full, preferred_element_type=jnp.float32)
    up_value = jnp.dot(x_rows, up_full, preferred_element_type=jnp.float32)
    grad_hidden = jnp.dot(dy_rows, down_full.T, preferred_element_type=jnp.float32)
    sigmoid_gate = jax.nn.sigmoid(pre_gate)
    grad_gate = (grad_hidden * up_value * sigmoid_gate * (1.0 + pre_gate * (1.0 - sigmoid_gate))).astype(jnp.bfloat16)
    grad_up = (grad_hidden * pre_gate * sigmoid_gate).astype(jnp.bfloat16)
    total = jnp.dot(grad_gate, gate_full.T, preferred_element_type=jnp.float32)
    total = total + jnp.dot(grad_up, up_full.T, preferred_element_type=jnp.float32)
    return total.astype(jnp.bfloat16)

def reference(hidden, cotangent, routes, gates, offsets, w_gate, w_up, w_down, w_out, latent, rope_key, q_nope, q_pe, w_uk, w_uv):
    blocks = TOKENS // TOK_DEV
    block_ids = routes.reshape(blocks, TOK_DEV * TOPK)
    slots = jax.vmap(partial(slot_numbers, experts=EXPERTS))(block_ids).reshape(-1)
    expert_flat = routes.reshape(-1).astype(jnp.int32)
    token_flat = jnp.repeat(jnp.arange(TOKENS, dtype=jnp.int32), TOPK)
    row_flat = (token_flat // TOK_DEV * CAP + slots).astype(jnp.int32)
    weighted = (gates.reshape(-1)[:, None] * cotangent[token_flat].astype(jnp.float32)).astype(jnp.bfloat16)
    zero_rows = jnp.zeros((EXPERTS, blocks * CAP, D), jnp.bfloat16)
    expert_in = zero_rows.at[expert_flat, row_flat].set(hidden[token_flat])
    expert_cot = zero_rows.at[expert_flat, row_flat].set(weighted)
    half_ffe = FFE // 2
    grads = lax.map(expert_grad, (expert_in, expert_cot, w_gate.reshape(EXPERTS, 2, D, half_ffe), w_up.reshape(EXPERTS, 2, D, half_ffe), w_down.reshape(EXPERTS, 2, half_ffe, D)))
    routed = grads[expert_flat, row_flat].astype(jnp.float32).reshape(TOKENS, TOPK, D).sum(axis=1)
    resid_grad = (cotangent.astype(jnp.float32) + routed).astype(jnp.bfloat16)
    score_scale = 1.0 / math.sqrt(NOPE + ROPE)
    grad_out = jnp.dot(resid_grad, w_out.T, preferred_element_type=jnp.float32).astype(jnp.bfloat16)
    local_steps = jnp.arange(TOK_WIDE, dtype=jnp.int32)
    position = (offsets[:, None] * TOK_WIDE + local_steps[None, :]).reshape(-1)
    visible = position[None, :] <= position[:, None]
    q_heads = q_nope.reshape(TOKENS, HEADS, NOPE).transpose(1, 0, 2)
    pe_heads = q_pe.reshape(TOKENS, HEADS, ROPE).transpose(1, 0, 2)
    out_heads = grad_out.reshape(TOKENS, HEADS, VDIM).transpose(1, 0, 2)
    uk_heads = w_uk.reshape(HEADS, NOPE, LATENT)
    uv_heads = w_uv.reshape(HEADS, VDIM, LATENT)

    def one_head(carry, inputs):
        q_one, pe_one, out_one, uk_one, uv_one = inputs
        query_latent = jnp.dot(q_one, uk_one, preferred_element_type=jnp.float32).astype(jnp.bfloat16)
        out_latent = jnp.dot(out_one, uv_one, preferred_element_type=jnp.float32).astype(jnp.bfloat16)
        scores = score_scale * (jnp.dot(query_latent, latent.T, preferred_element_type=jnp.float32) + jnp.dot(pe_one, rope_key.T, preferred_element_type=jnp.float32))
        masked = jnp.where(visible, scores, -1e+30)
        row_max = lax.optimization_barrier(jnp.max(masked, axis=1, keepdims=True))
        log_norm = row_max + jnp.log(lax.optimization_barrier(jnp.sum(jnp.exp(masked - row_max), axis=1, keepdims=True)))
        probs = jnp.exp(masked - log_norm)
        grad_probs = jnp.dot(out_latent, latent.T, preferred_element_type=jnp.float32)
        row_delta = lax.optimization_barrier(jnp.sum(probs * grad_probs, axis=1, keepdims=True))
        grad_scores = (score_scale * probs * (grad_probs - row_delta)).astype(jnp.bfloat16)
        probs_low = probs.astype(jnp.bfloat16)
        grad_qlat = jnp.dot(grad_scores, latent, preferred_element_type=jnp.float32).astype(jnp.bfloat16)
        grad_nope = jnp.dot(grad_qlat, uk_one.T, preferred_element_type=jnp.float32).astype(jnp.bfloat16)
        grad_pe = jnp.dot(grad_scores, rope_key, preferred_element_type=jnp.float32).astype(jnp.bfloat16)
        latent_sum = carry[0] + jnp.dot(probs_low.T, out_latent, preferred_element_type=jnp.float32)
        latent_sum = latent_sum + jnp.dot(grad_scores.T, query_latent, preferred_element_type=jnp.float32)
        rope_sum = carry[1] + jnp.dot(grad_scores.T, pe_one, preferred_element_type=jnp.float32)
        return ((latent_sum, rope_sum), (grad_nope, grad_pe))
    start = (jnp.zeros((TOKENS, LATENT), jnp.float32), jnp.zeros((TOKENS, ROPE), jnp.float32))
    sums, per_head = lax.scan(one_head, start, (q_heads, pe_heads, out_heads, uk_heads, uv_heads))
    grad_q_nope = per_head[0].transpose(1, 0, 2).reshape(TOKENS, HEADS * NOPE)
    grad_q_pe = per_head[1].transpose(1, 0, 2).reshape(TOKENS, HEADS * ROPE)
    return (resid_grad, grad_q_nope, grad_q_pe, sums[0], sums[1])
```

```python
import functools
import math

import jax
import jax.numpy as jnp
from jax import lax
from jax.experimental import pallas as pl
from jax.experimental.pallas import tpu as pltpu
from jax.sharding import PartitionSpec as P

LATENT = 512
NOPE = 128
ROPE = 64
VDIM = 128

F32 = jnp.float32
BF16 = jnp.bfloat16
CONTRACT_LAST = (((1,), (1,)), ((), ()))


def across(value, mask):
    pairs = [(source, source ^ mask) for source in range(lax.axis_size("wide"))]
    return lax.ppermute(value, "wide", pairs)


def along(value):
    size = lax.axis_size("narrow")
    return lax.ppermute(value, "narrow", [(i, (i + 1) % size) for i in range(size)])


def wide_levels():
    size = lax.axis_size("wide")
    masks = []
    mask = size // 2
    while mask:
        masks.append(mask)
        mask //= 2
    first, rest = masks[:2], masks[2:]
    return first, [rest[i : i + 2] for i in range(0, len(rest), 2)]


def gather_level(block, level):
    if len(level) == 1:
        return [block, across(block, level[0])]
    high, low = level
    by_low, by_high = across(block, low), across(block, high)
    half = block.shape[0] // 2
    corner = jnp.concatenate([across(by_low[:half], high), across(by_high[half:], low)], axis=0)
    return [block, by_low, by_high, corner]


def total(*terms):
    summed = terms[0].astype(F32)
    for term in terms[1:]:
        summed = summed + term.astype(F32)
    return summed.astype(BF16)


def scatter_level(blocks, level):
    if len(level) == 1:
        return total(blocks[0], across(blocks[1], level[0]))
    high, low = level
    own, by_low, by_high, corner = blocks
    half = own.shape[1] // 2
    from_high = across(corner[:, :half], high)
    from_low = across(corner[:, half:], low)
    by_low = jnp.concatenate([total(by_low[:, :half], from_high), by_low[:, half:]], axis=1)
    by_high = jnp.concatenate([by_high[:, :half], total(by_high[:, half:], from_low)], axis=1)
    return total(own, across(by_low, low), across(by_high, high))


def expert_kernel(count, gate_ref, *refs):
    tokens, (w_gate, w_up, w_down), outs = refs[:count], refs[count : count + 3], refs[count + 3 :]
    for index in range(count):
        pieces, _, rows, width = tokens[index].shape
        merged = pieces * rows
        x_rows = tokens[index][:, 0].reshape(merged, width)
        dy_rows = tokens[index][:, 1].reshape(merged, width)
        gate = gate_ref[pl.ds(index * merged, merged), :]
        pre_gate = jnp.dot(x_rows, w_gate[...], preferred_element_type=F32)
        up_value = jnp.dot(x_rows, w_up[...], preferred_element_type=F32)
        grad_hidden = gate * lax.dot_general(
            dy_rows, w_down[...], CONTRACT_LAST, preferred_element_type=F32
        )
        sigmoid_gate = jax.nn.sigmoid(pre_gate)
        grad_gate = grad_hidden * up_value * sigmoid_gate * (1.0 + pre_gate * (1.0 - sigmoid_gate))
        grad_up = grad_hidden * pre_gate * sigmoid_gate
        partial_grad = lax.dot_general(
            grad_gate.astype(BF16), w_gate[...], CONTRACT_LAST, preferred_element_type=F32
        )
        partial_grad = partial_grad + lax.dot_general(
            grad_up.astype(BF16), w_up[...], CONTRACT_LAST, preferred_element_type=F32
        )
        outs[index][...] = partial_grad.astype(BF16)


def expert_grads(tokens, gate, w_gate, w_up, w_down):
    count = len(tokens)
    pieces, _, rows, width = tokens[0].shape
    merged = pieces * rows
    flops = 2 * 5 * count * merged * width * w_gate.shape[1]
    return pl.pallas_call(
        functools.partial(expert_kernel, count),
        out_shape=[jax.ShapeDtypeStruct((merged, width), BF16)] * count,
        in_specs=[pl.BlockSpec(memory_space=pltpu.VMEM)] * (count + 4),
        out_specs=[pl.BlockSpec(memory_space=pltpu.VMEM)] * count,
        compiler_params=pltpu.CompilerParams(vmem_limit_bytes=40 * 2**20),
        cost_estimate=pl.CostEstimate(
            flops=flops, bytes_accessed=3 * w_gate.size * 2 + 6 * count * merged * width, transcendentals=0
        ),
    )(gate, *tokens, w_gate, w_up, w_down)


def routed_sum(hidden, cotangent, routes, gates, w_gate, w_up, w_down):
    rows, width = hidden.shape
    wide_size, ring = lax.axis_size("wide"), lax.axis_size("narrow")
    wide_index, ring_index = lax.axis_index("wide"), lax.axis_index("narrow")
    experts = wide_size * ring // 2
    expert = (wide_index * ring + ring_index) // 2
    named = routes[:, :, None] == jnp.arange(experts, dtype=jnp.int32)[None, None, :]
    dense = jnp.sum(jnp.where(named, gates[:, :, None], 0.0), axis=1)
    dense_all = lax.all_gather(dense, ("wide", "narrow"), axis=0, tiled=True)
    column = lax.dynamic_slice_in_dim(dense_all, expert, 1, 1).reshape(wide_size, ring, rows)

    (high, low), rest = wide_levels()
    corner_mask = high | low
    order = [0, low, high, corner_mask]
    for level in rest:
        extra = [0, level[0]] if len(level) == 1 else [0, level[1], level[0], level[0] | level[1]]
        order = [mask ^ more for more in extra for mask in order]
    places = wide_index ^ jnp.array(order, jnp.int32)

    own = jnp.concatenate([hidden, cotangent], axis=0)
    corner = None
    link_own = link_corner = None
    home = None
    for step in range(ring):
        if step:
            own = along(own)
        by_low, by_high = across(own, low), across(own, high)
        in_plane = step == 0 or step == ring - 1
        if in_plane:
            corner = jnp.concatenate(
                [across(by_low[:rows], high), across(by_high[rows:], low)], axis=0
            )
        else:
            corner = along(corner)
        blocks = [jnp.concatenate([own, by_low, by_high, corner], axis=0)]
        for level in rest:
            blocks = [piece for block in zip(*[gather_level(b, level) for b in blocks]) for piece in block]
        tokens = [block.reshape(4, 2, rows, width) for block in blocks]
        source = (ring_index - step) % ring
        gate = lax.dynamic_index_in_dim(column, source, 1, False)[places].reshape(-1, 1)
        partials = expert_grads(tokens, gate, w_gate, w_up, w_down)
        for level in reversed(rest):
            size = 2 ** len(level)
            group = len(partials) // size
            partials = [
                scatter_level([partials[i + group * j] for j in range(size)], level)
                for i in range(group)
            ]
        piece_own, piece_low, piece_high, piece_corner = partials[0].reshape(4, rows, width)
        if link_corner is not None:
            piece_corner = total(piece_corner, along(link_corner))
        if in_plane:
            summed = scatter_level([piece_own, piece_low, piece_high, piece_corner], (high, low))
            link_corner = None
        else:
            summed = total(piece_own, across(piece_low, low), across(piece_high, high))
            link_corner = piece_corner
        if step == 0:
            home = summed
        elif link_own is None:
            link_own = summed
        else:
            link_own = total(summed, along(link_own))
    return home.astype(F32) + along(link_own).astype(F32)


def on_device(
    hidden,
    cotangent,
    routes,
    gates,
    offsets,
    w_gate,
    w_up,
    w_down,
    w_out,
    latent,
    rope_key,
    q_nope,
    q_pe,
    w_uk,
    w_uv,
):
    routed = routed_sum(hidden, cotangent, routes, gates, w_gate[0], w_up[0], w_down[0])
    resid_grad = (cotangent.astype(jnp.float32) + routed).astype(jnp.bfloat16)
    contract_last = CONTRACT_LAST
    tok_wide = q_nope.shape[0]
    heads_local = q_nope.shape[1] // NOPE
    score_scale = 1.0 / math.sqrt(NOPE + ROPE)
    grad_out = lax.dot_general(
        lax.all_gather(resid_grad, "narrow", axis=0, tiled=True),
        w_out,
        contract_last,
        preferred_element_type=jnp.float32,
    ).astype(jnp.bfloat16)
    latent_all, rope_all = (
        lax.all_gather(latent, "wide", axis=0, tiled=True),
        lax.all_gather(rope_key, "wide", axis=0, tiled=True),
    )
    wide_index = lax.axis_index("wide")
    local_steps = jnp.arange(tok_wide, dtype=jnp.int32)
    query_pos = offsets[wide_index] * tok_wide + local_steps
    key_pos = (offsets[:, None] * tok_wide + local_steps[None, :]).reshape(-1)
    visible = key_pos[None, :] <= query_pos[:, None]
    q_heads = q_nope.reshape(tok_wide, heads_local, NOPE)
    pe_heads = q_pe.reshape(tok_wide, heads_local, ROPE)
    uk_heads = w_uk.reshape(heads_local, NOPE, LATENT)
    uv_heads = w_uv.reshape(heads_local, VDIM, LATENT)
    query_latent = jnp.einsum(
        "thn,hnl->htl", q_heads, uk_heads, preferred_element_type=jnp.float32
    ).astype(jnp.bfloat16)
    out_latent = jnp.einsum(
        "thv,hvl->htl",
        grad_out.reshape(tok_wide, heads_local, VDIM),
        uv_heads,
        preferred_element_type=jnp.float32,
    ).astype(jnp.bfloat16)
    scores = score_scale * (
        jnp.einsum("htl,sl->hts", query_latent, latent_all, preferred_element_type=jnp.float32)
        + jnp.einsum("thr,sr->hts", pe_heads, rope_all, preferred_element_type=jnp.float32)
    )
    masked = jnp.where(visible[None, :, :], scores, -1e30)
    row_max = jnp.max(masked, axis=2, keepdims=True)
    log_norm = row_max + jnp.log(jnp.sum(jnp.exp(masked - row_max), axis=2, keepdims=True))
    probs = jnp.exp(masked - log_norm)
    grad_probs = jnp.einsum(
        "htl,sl->hts", out_latent, latent_all, preferred_element_type=jnp.float32
    )
    row_delta = jnp.sum(probs * grad_probs, axis=2, keepdims=True)
    grad_scores = (score_scale * probs * (grad_probs - row_delta)).astype(jnp.bfloat16)
    probs_low = probs.astype(jnp.bfloat16)
    grad_qlat = jnp.einsum(
        "hts,sl->htl", grad_scores, latent_all, preferred_element_type=jnp.float32
    ).astype(jnp.bfloat16)
    grad_q_nope = jnp.einsum(
        "htl,hnl->thn", grad_qlat, uk_heads, preferred_element_type=jnp.float32
    )
    grad_q_nope = grad_q_nope.astype(jnp.bfloat16).reshape(tok_wide, heads_local * NOPE)
    grad_q_pe = jnp.einsum("hts,sr->thr", grad_scores, rope_all, preferred_element_type=jnp.float32)
    grad_q_pe = grad_q_pe.astype(jnp.bfloat16).reshape(tok_wide, heads_local * ROPE)
    latent_term = jnp.einsum(
        "hts,htl->sl", probs_low, out_latent, preferred_element_type=jnp.float32
    )
    latent_term = latent_term + jnp.einsum(
        "hts,htl->sl", grad_scores, query_latent, preferred_element_type=jnp.float32
    )
    rope_term = jnp.einsum("hts,thr->sr", grad_scores, pe_heads, preferred_element_type=jnp.float32)
    block_latent, block_rope = jax.tree.map(
        lambda part: lax.psum_scatter(
            part.astype(jnp.bfloat16), "wide", scatter_dimension=0, tiled=True
        ).astype(jnp.float32),
        (latent_term, rope_term),
    )
    grad_latent, grad_rope_key = (
        lax.psum_scatter(
            block_latent.astype(jnp.bfloat16), "narrow", scatter_dimension=0, tiled=True
        ).astype(jnp.float32),
        lax.psum_scatter(
            block_rope.astype(jnp.bfloat16), "narrow", scatter_dimension=0, tiled=True
        ).astype(jnp.float32),
    )
    return (resid_grad, grad_q_nope, grad_q_pe, grad_latent, grad_rope_key)


def solution(mesh):
    return jax.shard_map(
        on_device,
        mesh=mesh,
        in_specs=(
            P(("wide", "narrow"), None),
            P(("wide", "narrow"), None),
            P(("wide", "narrow"), None),
            P(("wide", "narrow"), None),
            P(),
            P(("wide", "narrow"), None, None),
            P(("wide", "narrow"), None, None),
            P(("wide", "narrow"), None, None),
            P("narrow", None),
            P("wide", None),
            P("wide", None),
            P("wide", "narrow"),
            P("wide", "narrow"),
            P("narrow", None),
            P("narrow", None),
        ),
        out_specs=(
            P(("wide", "narrow"), None),
            P("wide", "narrow"),
            P("wide", "narrow"),
            P(("wide", "narrow"), None),
            P(("wide", "narrow"), None),
        ),
        check_vma=False,
    )
```

```python
import functools
import math

import jax
import jax.numpy as jnp
from jax import lax
from jax.experimental import pallas as pl
from jax.experimental.pallas import tpu as pltpu
from jax.sharding import PartitionSpec as P

LATENT = 512
NOPE = 128
ROPE = 64
VDIM = 128

F32 = jnp.float32
BF16 = jnp.bfloat16
CONTRACT_LAST = (((1,), (1,)), ((), ()))


def across(value, mask):
    pairs = [(source, source ^ mask) for source in range(lax.axis_size("wide"))]
    return lax.ppermute(value, "wide", pairs)


def along(value):
    size = lax.axis_size("narrow")
    return lax.ppermute(value, "narrow", [(i, (i + 1) % size) for i in range(size)])


def wide_levels():
    size = lax.axis_size("wide")
    masks = []
    mask = size // 2
    while mask:
        masks.append(mask)
        mask //= 2
    first, rest = masks[:2], masks[2:]
    return first, [rest[i : i + 2] for i in range(0, len(rest), 2)]


def gather_level(block, level):
    if len(level) == 1:
        return [block, across(block, level[0])]
    high, low = level
    by_low, by_high = across(block, low), across(block, high)
    half = block.shape[0] // 2
    corner = jnp.concatenate([across(by_low[:half], high), across(by_high[half:], low)], axis=0)
    return [block, by_low, by_high, corner]


def total(*terms):
    summed = terms[0].astype(F32)
    for term in terms[1:]:
        summed = summed + term.astype(F32)
    return summed.astype(BF16)


def scatter_level(blocks, level):
    if len(level) == 1:
        return total(blocks[0], across(blocks[1], level[0]))
    high, low = level
    own, by_low, by_high, corner = blocks
    half = own.shape[1] // 2
    from_high = across(corner[:, :half], high)
    from_low = across(corner[:, half:], low)
    by_low = jnp.concatenate([total(by_low[:, :half], from_high), by_low[:, half:]], axis=1)
    by_high = jnp.concatenate([by_high[:, :half], total(by_high[:, half:], from_low)], axis=1)
    return total(own, across(by_low, low), across(by_high, high))

LANES = 128
VMEM = pl.BlockSpec(memory_space=pltpu.VMEM)
SMEM = pl.BlockSpec(memory_space=pltpu.SMEM)


def dot(left, right):
    return jnp.dot(left, right, preferred_element_type=F32)


def dot_last(left, right):
    return lax.dot_general(left, right, CONTRACT_LAST, preferred_element_type=F32)


def call(kernel, outs, ins, flops, limit=48):
    specs = [entry[1] if isinstance(entry, tuple) else VMEM for entry in ins]
    arrays = [entry[0] if isinstance(entry, tuple) else entry for entry in ins]
    moved = sum(math.prod(out.shape) * out.dtype.itemsize for out in outs)
    moved += sum(array.size * array.dtype.itemsize for array in arrays)
    return pl.pallas_call(
        kernel,
        out_shape=outs,
        in_specs=specs,
        out_specs=[VMEM] * len(outs),
        compiler_params=pltpu.CompilerParams(vmem_limit_bytes=limit * 2**20),
        cost_estimate=pl.CostEstimate(flops=flops, bytes_accessed=moved, transcendentals=0),
    )(*arrays)


def pack_kernel(experts, hidden, cotangent, routes, gates, latent, rope, out):
    rows, width = hidden.shape
    half = latent.shape[1] // 2
    tail = out.shape[2] - width - half
    out[0, :, :width] = hidden[...]
    out[1, :, :width] = cotangent[...]
    out[0, :, width : width + half] = latent[:, :half]
    out[1, :, width : width + half] = latent[:, half:]
    out[0, :, width + half :] = jnp.zeros((rows, tail), BF16)
    out[0, :, width + half : width + half + rope.shape[1]] = rope[...]
    lane = lax.broadcasted_iota(jnp.int32, (rows, tail), 1)
    first = jnp.zeros((rows, tail), F32)
    second = jnp.zeros((rows, tail), F32)
    for k in range(routes.shape[1]):
        chosen, weight = routes[:, k : k + 1], gates[:, k : k + 1]
        first = first + jnp.where(lane == chosen, weight, 0.0)
        second = second + jnp.where(lane == chosen + experts, weight, 0.0)
    second = second - second.astype(BF16).astype(F32)
    out[1, :, width + half :] = (first + second).astype(BF16)


def expert_kernel(count, experts, expert_ref, *refs):
    tokens, (w_gate, w_up, w_down) = refs[:count], refs[count : count + 3]
    keys, outs = refs[count + 3], refs[count + 4 :]
    width = w_down.shape[1]
    for index in range(count):
        pieces, _, rows, wide = tokens[index].shape
        merged = pieces * rows
        tail = keys.shape[1] - LATENT
        half = wide - tail
        here = pl.ds(index * merged, merged)
        x_rows = tokens[index][:, 0, :, :width].reshape(merged, width)
        dy_rows = tokens[index][:, 1, :, :width].reshape(merged, width)
        keys[here, : half - width] = tokens[index][:, 0, :, width:half].reshape(merged, half - width)
        keys[here, half - width : LATENT] = tokens[index][:, 1, :, width:half].reshape(
            merged, half - width
        )
        keys[here, LATENT:] = tokens[index][:, 0, :, half:].reshape(merged, tail)
        parts = tokens[index][:, 1, :, half:].reshape(merged, tail).astype(F32)
        lane = lax.broadcasted_iota(jnp.int32, (merged, tail), 1)
        mine = (lane == expert_ref[0]) | (lane == expert_ref[0] + experts)
        gate = jnp.sum(jnp.where(mine, parts, 0.0), axis=1, keepdims=True)
        pre_gate = dot_last(x_rows, w_gate[...])
        up_value = dot_last(x_rows, w_up[...])
        grad_hidden = gate * dot_last(dy_rows, w_down[...])
        sigmoid_gate = jax.nn.sigmoid(pre_gate)
        scaled = grad_hidden * sigmoid_gate
        grad_gate = scaled * up_value * (1.0 + pre_gate * (1.0 - sigmoid_gate))
        grad_up = scaled * pre_gate
        partial_grad = dot(grad_gate.astype(BF16), w_gate[...])
        partial_grad = partial_grad + dot(grad_up.astype(BF16), w_up[...])
        outs[index][...] = partial_grad.astype(BF16)


def expert_grads(expert, experts, tokens, w_gate, w_up, w_down):
    count = len(tokens)
    pieces, _, rows, wide = tokens[0].shape
    merged, width = pieces * rows, w_down.shape[1]
    key_width = LATENT + wide - width - LATENT // 2
    out = jax.ShapeDtypeStruct((merged, width), BF16)
    result = call(
        functools.partial(expert_kernel, count, experts),
        [jax.ShapeDtypeStruct((count * merged, key_width), BF16)] + [out] * count,
        [(expert, SMEM), *tokens, w_gate, w_up, w_down],
        10 * count * merged * w_gate.size,
    )
    return result[0], result[1:]


def after(value, *earlier):
    return lax.optimization_barrier((value, *earlier))[0]


def routed_sum(payload, rows, w_gate, w_up, w_down):
    wide_size, ring = lax.axis_size("wide"), lax.axis_size("narrow")
    wide_index, ring_index = lax.axis_index("wide"), lax.axis_index("narrow")
    experts = wide_size * ring // 2
    expert = ((wide_index * ring + ring_index) // 2).astype(jnp.int32).reshape(1)
    wide, width = payload.shape[1], w_down.shape[1]
    (high, low), rest = wide_levels()

    own = payload
    corner = None
    columns = []
    for step in range(ring):
        columns.append(own)
        own = along(own) if step < ring - 1 else None
    link_own = link_corner = home = None
    all_keys, done = [], []
    for step in range(ring):
        own = columns[step]
        if step >= 2:
            own = after(own, done[step - 2])
        by_low, by_high = across(own, low), across(own, high)
        in_plane = step == 0 or step >= ring - 2
        if in_plane:
            corner = jnp.concatenate(
                [across(by_low[:rows], high), across(by_high[rows:], low)], axis=0
            )
        else:
            corner = along(corner)
        blocks = [jnp.concatenate([own, by_low, by_high, corner], axis=0)]
        for level in rest:
            blocks = [piece for block in zip(*[gather_level(b, level) for b in blocks]) for piece in block]
        tokens = [block.reshape(4, 2, rows, wide) for block in blocks]
        keys, partials = expert_grads(expert, experts, tokens, w_gate, w_up, w_down)
        all_keys.append(keys)
        done.append(partials[0])
        for level in reversed(rest):
            size = 2 ** len(level)
            group = len(partials) // size
            partials = [
                scatter_level([partials[i + group * j] for j in range(size)], level)
                for i in range(group)
            ]
        piece_own, piece_low, piece_high, piece_corner = partials[0].reshape(4, rows, width)
        if link_corner is not None:
            piece_corner = total(piece_corner, along(link_corner))
        if in_plane:
            summed = scatter_level([piece_own, piece_low, piece_high, piece_corner], (high, low))
            link_corner = None
        else:
            summed = total(piece_own, across(piece_low, low), across(piece_high, high))
            link_corner = piece_corner
        if step == 0:
            home = summed
        elif link_own is None:
            link_own = summed
        else:
            link_own = total(summed, along(link_own))
    return home.astype(F32) + along(link_own).astype(F32), all_keys


def before_kernel(slabs, heads, scale, bases, query_base, q_nope, q_pe, w_uk, *refs):
    keys, (queries, outs_t), rest = refs[:slabs], refs[slabs : slabs + 2], refs[slabs + 2 :]
    probs, keys_t, scores, queries_t = rest[:slabs], rest[slabs : 2 * slabs], rest[2 * slabs], rest[2 * slabs + 1]
    tok = q_nope.shape[0]
    key_count, key_width = keys[0].shape
    columns = heads * tok
    pieces = bases.shape[1]
    rows = key_count // pieces
    queries[:, LATENT:] = jnp.zeros((columns, key_width - LATENT), BF16)
    for head in range(heads):
        here = pl.ds(head * tok, tok)
        queries[here, :LATENT] = dot(
            q_nope[:, head * NOPE : (head + 1) * NOPE], w_uk[head * NOPE : (head + 1) * NOPE, :]
        ).astype(BF16)
        queries[here, LATENT : LATENT + ROPE] = q_pe[:, head * ROPE : (head + 1) * ROPE]
        queries_t[:, here] = queries[here, :].T
    position = query_base[0] + lax.rem(
        lax.broadcasted_iota(jnp.int32, (rows, columns), 1), jnp.int32(tok)
    )
    step = lax.broadcasted_iota(jnp.int32, (rows, columns), 0)
    ahead = step - position
    top = jnp.full((1, columns), -1e30, F32)
    for slab in range(slabs):
        raw = dot(keys[slab][...], queries_t[...])
        for piece in range(pieces):
            shown = ahead + bases[slab, piece] <= 0
            masked = jnp.where(shown, raw[piece * rows : (piece + 1) * rows, :] * scale, -1e30)
            scores[pl.ds(slab * key_count + piece * rows, rows), :] = masked
            top = jnp.maximum(top, jnp.max(masked, axis=0, keepdims=True))
        keys_t[slab][...] = keys[slab][...].T
    norm = jnp.zeros((1, columns), F32)
    for slab in range(slabs):
        here = pl.ds(slab * key_count, key_count)
        grown = jnp.exp(scores[here, :] - top)
        scores[here, :] = grown
        norm = norm + jnp.sum(grown, axis=0, keepdims=True)
    inverse = 1.0 / norm
    for slab in range(slabs):
        here = pl.ds(slab * key_count, key_count)
        probs[slab][...] = (scores[here, :] * inverse).astype(BF16)
        part = dot(keys_t[slab][:LATENT, :], probs[slab][...])
        if slab == 0:
            outs_t[...] = part
        else:
            outs_t[...] += part


def key_kernel(slabs, heads, count, scale, index, w_out, w_uv, queries, outs_t, *refs):
    resid, refs = refs[:slabs], refs[slabs:]
    keys, probs, refs = refs[:slabs], refs[slabs : 2 * slabs], refs[2 * slabs :]
    grads, terms, (grad_out, latents, latents_t) = refs[:slabs], refs[slabs : slabs + count], refs[slabs + count :]
    rows = resid[0].shape[0]
    tok = rows * slabs
    key_count, key_width = keys[0].shape
    for slab in range(slabs):
        place = lax.rem(index[0] + (slabs - slab), jnp.int32(slabs))
        grad_out[pl.ds(pl.multiple_of(place * rows, rows), rows), :] = dot_last(
            resid[slab][...], w_out[...]
        ).astype(BF16)
    for head in range(heads):
        here = pl.ds(head * tok, tok)
        latents[here, :] = dot(
            grad_out[:, head * VDIM : (head + 1) * VDIM], w_uv[head * VDIM : (head + 1) * VDIM, :]
        ).astype(BF16)
        latents_t[:, here] = latents[here, :].T
    delta = jnp.sum(outs_t[...] * latents_t[...].astype(F32), axis=0, keepdims=True)
    share = key_count // count
    for slab in range(slabs):
        grad_probs = dot(keys[slab][:, :LATENT], latents_t[...])
        grads[slab][...] = (
            scale * probs[slab][...].astype(F32) * (grad_probs - delta)
        ).astype(BF16)
        term = dot(grads[slab][...], queries[...])
        term_latent = term[:, :LATENT] + dot(probs[slab][...], latents[...])
        for block in range(count):
            part = slice(block * share, (block + 1) * share)
            pieces = terms[block].shape[0]
            terms[block][:, slab, :, :LATENT] = (
                term_latent[part].astype(BF16).reshape(pieces, rows, LATENT)
            )
            terms[block][:, slab, :, LATENT:] = (
                term[part, LATENT:].astype(BF16).reshape(pieces, rows, key_width - LATENT)
            )


def query_kernel(slabs, heads, w_uk, *refs):
    keys_t, grads, (grad_nope, grad_pe) = refs[:slabs], refs[slabs : 2 * slabs], refs[2 * slabs :]
    tok = grad_nope.shape[0]
    summed = dot(keys_t[0][...], grads[0][...])
    for slab in range(1, slabs):
        summed = summed + dot(keys_t[slab][...], grads[slab][...])
    for head in range(heads):
        here = slice(head * tok, (head + 1) * tok)
        grad_latent = summed[:LATENT, here].astype(BF16)
        nope = dot(w_uk[head * NOPE : (head + 1) * NOPE, :], grad_latent)
        grad_nope[:, head * NOPE : (head + 1) * NOPE] = nope.T.astype(BF16)
        grad_pe[:, head * ROPE : (head + 1) * ROPE] = summed[LATENT : LATENT + ROPE, here].T.astype(BF16)


def on_device(
    hidden,
    cotangent,
    routes,
    gates,
    offsets,
    w_gate,
    w_up,
    w_down,
    w_out,
    latent,
    rope_key,
    q_nope,
    q_pe,
    w_uk,
    w_uv,
):
    rows, width = hidden.shape
    tok = q_nope.shape[0]
    heads = q_nope.shape[1] // NOPE
    scale = 1.0 / math.sqrt(NOPE + ROPE)
    wide_size, ring = lax.axis_size("wide"), lax.axis_size("narrow")
    wide_index, ring_index = lax.axis_index("wide"), lax.axis_index("narrow")
    experts = wide_size * ring // 2
    (high, low), rest = wide_levels()
    key_width = LATENT + -(-max(ROPE, 2 * experts) // LANES) * LANES
    latent_own = lax.dynamic_slice_in_dim(latent, ring_index * rows, rows, 0)
    rope_own = lax.dynamic_slice_in_dim(rope_key, ring_index * rows, rows, 0)
    (payload,) = call(
        functools.partial(pack_kernel, experts),
        [jax.ShapeDtypeStruct((2, rows, width + key_width - LATENT // 2), BF16)],
        [hidden, cotangent, routes, gates, latent_own, rope_own],
        0,
        8,
    )
    payload = payload.reshape(2 * rows, -1)
    routed, keys = routed_sum(payload, rows, w_gate[0].T, w_up[0].T, w_down[0])
    resid_grad = (cotangent.astype(F32) + routed).astype(BF16)

    order = [0, low, high, high | low]
    for level in rest:
        extra = [0, level[0]] if len(level) == 1 else [0, level[1], level[0], level[0] | level[1]]
        order = [mask ^ more for more in extra for mask in order]
    places = wide_index ^ jnp.array(order, jnp.int32)
    turns = (ring_index - jnp.arange(ring, dtype=jnp.int32)) % ring
    bases = offsets[places][None, :] * tok + turns[:, None] * rows
    query_base = (offsets[wide_index] * tok).reshape(1)

    columns, key_count = heads * tok, keys[0].shape[0]
    shape = jax.ShapeDtypeStruct
    made = pl.pallas_call(
        functools.partial(before_kernel, ring, heads, scale),
        out_shape=[shape((columns, key_width), BF16), shape((LATENT, columns), F32)]
        + [shape((key_count, columns), BF16)] * ring
        + [shape((key_width, key_count), BF16)] * ring,
        in_specs=[SMEM, SMEM] + [VMEM] * (3 + ring),
        out_specs=[VMEM] * (2 + 2 * ring),
        scratch_shapes=[pltpu.VMEM((ring * key_count, columns), F32), pltpu.VMEM((key_width, columns), BF16)],
        compiler_params=pltpu.CompilerParams(vmem_limit_bytes=48 * 2**20),
        cost_estimate=pl.CostEstimate(
            flops=4 * ring * key_count * columns * key_width, bytes_accessed=10**7, transcendentals=ring * key_count * columns
        ),
    )(bases, query_base, q_nope, q_pe, w_uk, *keys)
    queries, outs_t, probs, keys_t = made[0], made[1], made[2 : 2 + ring], made[2 + ring :]

    pieces = [resid_grad]
    for _ in range(ring - 1):
        pieces.append(along(pieces[-1]))
    count = math.prod(2 ** len(level) for level in rest)
    made = pl.pallas_call(
        functools.partial(key_kernel, ring, heads, count, scale),
        out_shape=[shape((key_count, columns), BF16)] * ring
        + [shape((4, ring, rows, key_width), BF16)] * count,
        in_specs=[SMEM] + [VMEM] * (4 + 3 * ring),
        out_specs=[VMEM] * (ring + count),
        scratch_shapes=[
            pltpu.VMEM((tok, heads * VDIM), BF16),
            pltpu.VMEM((columns, LATENT), BF16),
            pltpu.VMEM((LATENT, columns), BF16),
        ],
        compiler_params=pltpu.CompilerParams(vmem_limit_bytes=48 * 2**20),
        cost_estimate=pl.CostEstimate(
            flops=6 * ring * key_count * columns * key_width, bytes_accessed=10**7, transcendentals=0
        ),
    )(ring_index.astype(jnp.int32).reshape(1), w_out, w_uv, queries, outs_t, *pieces, *keys, *probs)
    grads, terms = made[:ring], made[ring:]
    grad_q_nope, grad_q_pe = call(
        functools.partial(query_kernel, ring, heads),
        [shape(q_nope.shape, BF16), shape(q_pe.shape, BF16)],
        [w_uk, *keys_t, *grads],
        2 * ring * key_count * columns * key_width,
    )

    for level in reversed(rest):
        size = 2 ** len(level)
        group = len(terms) // size
        terms = [
            total(
                *[
                    terms[i] if j == 0 else across(terms[i + group * j], mask)
                    for j, mask in enumerate([0, *level] if size == 2 else [0, level[1], level[0], level[0] | level[1]])
                ]
            )
            for i in range(group)
        ]
    own, by_low, by_high, corner = terms[0]
    own = total(own, across(by_low, low), across(by_high, high), across(corner, high | low))
    key_grad = own[0].astype(F32)
    for step in range(1, ring):
        moves = [(i, (i - step) % ring) for i in range(ring)]
        key_grad = key_grad + lax.ppermute(own[step], "narrow", moves).astype(F32)
    return (
        resid_grad,
        grad_q_nope,
        grad_q_pe,
        key_grad[:, :LATENT],
        key_grad[:, LATENT : LATENT + ROPE],
    )


def solution(mesh):
    return jax.shard_map(
        on_device,
        mesh=mesh,
        in_specs=(
            P(("wide", "narrow"), None),
            P(("wide", "narrow"), None),
            P(("wide", "narrow"), None),
            P(("wide", "narrow"), None),
            P(),
            P(("wide", "narrow"), None, None),
            P(("wide", "narrow"), None, None),
            P(("wide", "narrow"), None, None),
            P("narrow", None),
            P("wide", None),
            P("wide", None),
            P("wide", "narrow"),
            P("wide", "narrow"),
            P("narrow", None),
            P("narrow", None),
        ),
        out_specs=(
            P(("wide", "narrow"), None),
            P("wide", "narrow"),
            P("wide", "narrow"),
            P(("wide", "narrow"), None),
            P(("wide", "narrow"), None),
        ),
        check_vma=False,
    )
```

```python
import functools
import math

import jax
import jax.numpy as jnp
from jax import lax
from jax.experimental import pallas as pl
from jax.experimental.pallas import tpu as pltpu
from jax.sharding import PartitionSpec as P

LATENT = 512
NOPE = 128
ROPE = 64
VDIM = 128

F32 = jnp.float32
BF16 = jnp.bfloat16
CONTRACT_LAST = (((1,), (1,)), ((), ()))


def across(value, mask):
    pairs = [(source, source ^ mask) for source in range(lax.axis_size("wide"))]
    return lax.ppermute(value, "wide", pairs)


def along(value):
    size = lax.axis_size("narrow")
    return lax.ppermute(value, "narrow", [(i, (i + 1) % size) for i in range(size)])


def wide_levels():
    size = lax.axis_size("wide")
    masks = []
    mask = size // 2
    while mask:
        masks.append(mask)
        mask //= 2
    first, rest = masks[:2], masks[2:]
    return first, [rest[i : i + 2] for i in range(0, len(rest), 2)]


def gather_level(block, level):
    if len(level) == 1:
        return [block, across(block, level[0])]
    high, low = level
    by_low, by_high = across(block, low), across(block, high)
    half = block.shape[0] // 2
    corner = jnp.concatenate([across(by_low[:half], high), across(by_high[half:], low)], axis=0)
    return [block, by_low, by_high, corner]


def total(*terms):
    summed = terms[0].astype(F32)
    for term in terms[1:]:
        summed = summed + term.astype(F32)
    return summed.astype(BF16)


def scatter_level(blocks, level):
    if len(level) == 1:
        return total(blocks[0], across(blocks[1], level[0]))
    high, low = level
    own, by_low, by_high, corner = blocks
    half = own.shape[1] // 2
    from_high = across(corner[:, :half], high)
    from_low = across(corner[:, half:], low)
    by_low = jnp.concatenate([total(by_low[:, :half], from_high), by_low[:, half:]], axis=1)
    by_high = jnp.concatenate([by_high[:, :half], total(by_high[:, half:], from_low)], axis=1)
    return total(own, across(by_low, low), across(by_high, high))

LANES = 128
VMEM = pl.BlockSpec(memory_space=pltpu.VMEM)
SMEM = pl.BlockSpec(memory_space=pltpu.SMEM)


def dot(left, right):
    return jnp.dot(left, right, preferred_element_type=F32)


def dot_last(left, right):
    return lax.dot_general(left, right, CONTRACT_LAST, preferred_element_type=F32)


def call(kernel, outs, ins, flops, limit, scratch=()):
    specs = [entry[1] if isinstance(entry, tuple) else VMEM for entry in ins]
    arrays = [entry[0] if isinstance(entry, tuple) else entry for entry in ins]
    moved = sum(math.prod(out.shape) * out.dtype.itemsize for out in outs)
    moved += sum(array.size * array.dtype.itemsize for array in arrays)
    return pl.pallas_call(
        kernel,
        out_shape=outs,
        in_specs=specs,
        out_specs=[VMEM] * len(outs),
        scratch_shapes=list(scratch),
        compiler_params=pltpu.CompilerParams(vmem_limit_bytes=limit * 2**20),
        cost_estimate=pl.CostEstimate(flops=flops, bytes_accessed=moved, transcendentals=0),
    )(*arrays)


def pack_kernel(experts, index, hidden, cotangent, routes, gates, latent, rope, out, turned):
    rows, width = hidden.shape
    half = latent.shape[1] // 2
    tail = out.shape[2] - width - half
    place = pl.ds(pl.multiple_of(index[0] * rows, rows), rows)
    out[0, :, :width] = hidden[...]
    out[1, :, :width] = cotangent[...]
    out[0, :, width : width + half] = latent[place, :half]
    out[1, :, width : width + half] = latent[place, half:]
    turned[...] = rope[...].T
    out[0, :, width + half :] = jnp.zeros((rows, tail), BF16)
    out[0, :, width + half : width + half + ROPE] = turned[place, :]
    line = lax.broadcasted_iota(jnp.int32, (tail, rows), 0)
    first = jnp.zeros((tail, rows), F32)
    second = jnp.zeros((tail, rows), F32)
    for k in range(routes.shape[0]):
        chosen, weight = routes[k : k + 1, :], gates[k : k + 1, :]
        first = first + jnp.where(line == chosen, weight, 0.0)
        second = second + jnp.where(line == chosen + experts, weight, 0.0)
    second = second - second.astype(BF16).astype(F32)
    out[1, :, width + half :] = (first + second).T.astype(BF16)


def expert_kernel(count, experts, expert_ref, *refs):
    tokens, (w_gate, w_up, w_down) = refs[:count], refs[count : count + 3]
    keys, outs = refs[count + 3], refs[count + 4 :]
    width = w_down.shape[1]
    for index in range(count):
        pieces, _, rows, wide = tokens[index].shape
        merged = pieces * rows
        tail = keys.shape[1] - LATENT
        half = wide - tail
        here = pl.ds(index * merged, merged)
        x_rows = tokens[index][:, 0, :, :width].reshape(merged, width)
        dy_rows = tokens[index][:, 1, :, :width].reshape(merged, width)
        keys[here, : half - width] = tokens[index][:, 0, :, width:half].reshape(merged, half - width)
        keys[here, half - width : LATENT] = tokens[index][:, 1, :, width:half].reshape(
            merged, half - width
        )
        keys[here, LATENT:] = tokens[index][:, 0, :, half:].reshape(merged, tail)
        parts = tokens[index][:, 1, :, half:].reshape(merged, tail).astype(F32)
        lane = lax.broadcasted_iota(jnp.int32, (merged, tail), 1)
        mine = (lane == expert_ref[0]) | (lane == expert_ref[0] + experts)
        gate = jnp.sum(jnp.where(mine, parts, 0.0), axis=1, keepdims=True)
        pre_gate = dot_last(x_rows, w_gate[...])
        up_value = dot_last(x_rows, w_up[...])
        grad_hidden = gate * dot_last(dy_rows, w_down[...])
        sigmoid_gate = jax.nn.sigmoid(pre_gate)
        scaled = grad_hidden * sigmoid_gate
        grad_gate = scaled * up_value * (1.0 + pre_gate * (1.0 - sigmoid_gate))
        grad_up = scaled * pre_gate
        both = jnp.concatenate([grad_gate.astype(BF16), grad_up.astype(BF16)], axis=1)
        weights = jnp.concatenate([w_gate[...], w_up[...]], axis=0)
        outs[index][...] = dot(both, weights).astype(BF16)


def expert_grads(expert, experts, tokens, w_gate, w_up, w_down):
    count = len(tokens)
    pieces, _, rows, wide = tokens[0].shape
    merged, width = pieces * rows, w_down.shape[1]
    key_width = LATENT + wide - width - LATENT // 2
    out = jax.ShapeDtypeStruct((merged, width), BF16)
    result = call(
        functools.partial(expert_kernel, count, experts),
        [jax.ShapeDtypeStruct((count * merged, key_width), BF16)] + [out] * count,
        [(expert, SMEM), *tokens, w_gate, w_up, w_down],
        10 * count * merged * w_gate.size,
        30,
    )
    return result[0], result[1:]


def after(value, *earlier):
    return lax.optimization_barrier((value, *earlier))[0]


def routed_sum(payload, rows, w_gate, w_up, w_down):
    wide_size, ring = lax.axis_size("wide"), lax.axis_size("narrow")
    wide_index, ring_index = lax.axis_index("wide"), lax.axis_index("narrow")
    experts = wide_size * ring // 2
    expert = ((wide_index * ring + ring_index) // 2).astype(jnp.int32).reshape(1)
    wide, width = payload.shape[1], w_down.shape[1]
    (high, low), rest = wide_levels()

    def in_plane(step):
        return step == 0 or step >= ring - 2

    columns = [payload]
    planes = []

    def spread(step):
        planes.append((across(columns[step], low), across(columns[step], high)))

    corner = link_own = link_corner = home = None
    all_keys, partials, halves = [], None, None
    columns.append(along(columns[0]))
    spread(0)
    halves = (across(planes[0][0][:rows], high), across(planes[0][1][rows:], low))
    columns.append(along(columns[1]))
    spread(1)
    for step in range(ring):
        by_low, by_high = planes[step]
        if in_plane(step):
            corner = jnp.concatenate(list(halves), axis=0)
        else:
            corner = along(corner)
            if step + 2 < ring:
                columns.append(along(after(columns[step + 1], corner)))
        if step:
            by_low, by_high, corner, _ = lax.optimization_barrier(
                (by_low, by_high, corner, partials[0])
            )
        blocks = [jnp.concatenate([columns[step], by_low, by_high, corner], axis=0)]
        for level in rest:
            blocks = [piece for block in zip(*[gather_level(b, level) for b in blocks]) for piece in block]
        if step + 2 < ring:
            if step == 0:
                blocks[0] = after(blocks[0], columns[2])
            spread(step + 2)
        if step + 1 < ring and in_plane(step + 1):
            blocks[0] = after(blocks[0], *planes[step + 1])
            halves = (across(planes[step + 1][0][:rows], high), across(planes[step + 1][1][rows:], low))
        tokens = [block.reshape(4, 2, rows, wide) for block in blocks]
        keys, partials = expert_grads(expert, experts, tokens, w_gate, w_up, w_down)
        all_keys.append(keys)
        sums = partials
        for level in reversed(rest):
            size = 2 ** len(level)
            group = len(sums) // size
            sums = [
                scatter_level([sums[i + group * j] for j in range(size)], level)
                for i in range(group)
            ]
        piece_own, piece_low, piece_high, piece_corner = sums[0].reshape(4, rows, width)
        if link_corner is not None:
            piece_corner = total(piece_corner, along(link_corner))
        if in_plane(step):
            summed = scatter_level([piece_own, piece_low, piece_high, piece_corner], (high, low))
            link_corner = None
        else:
            summed = total(piece_own, across(piece_low, low), across(piece_high, high))
            link_corner = piece_corner
        if step == 0:
            home = summed
        elif link_own is None:
            link_own = summed
        else:
            link_own = total(summed, along(link_own))
    return home.astype(F32) + along(link_own).astype(F32), all_keys


def score_kernel(heads, scale, bases, query_base, q_nope, q_pe, w_uk, *refs):
    slabs, pieces = bases.shape
    keys, (queries, top, *rest), queries_t = refs[:slabs], refs[slabs:-1], refs[-1]
    scores, keys_t = rest[:slabs], rest[slabs:]
    tok = q_nope.shape[0]
    key_count, key_width = keys[0].shape
    columns = heads * tok
    rows = key_count // pieces
    queries[:, LATENT:] = jnp.zeros((columns, key_width - LATENT), BF16)
    for head in range(heads):
        here = pl.ds(head * tok, tok)
        queries[here, :LATENT] = dot(
            q_nope[:, head * NOPE : (head + 1) * NOPE], w_uk[head * NOPE : (head + 1) * NOPE, :]
        ).astype(BF16)
        queries[here, LATENT : LATENT + ROPE] = q_pe[:, head * ROPE : (head + 1) * ROPE]
        queries_t[:, here] = queries[here, :].T
    position = query_base[0] + lax.rem(
        lax.broadcasted_iota(jnp.int32, (rows, columns), 1), jnp.int32(tok)
    )
    ahead = lax.broadcasted_iota(jnp.int32, (rows, columns), 0) - position
    highest = jnp.full((1, columns), -1e30, F32)
    for slab in range(slabs):
        raw = dot(keys[slab][...], queries_t[...])
        for piece in range(pieces):
            here = slice(piece * rows, (piece + 1) * rows)
            shown = ahead + bases[slab, piece] <= 0
            masked = jnp.where(shown, raw[here, :] * scale, -1e30)
            scores[slab][here, :] = masked
            highest = jnp.maximum(highest, jnp.max(masked, axis=0, keepdims=True))
        keys_t[slab][...] = keys[slab][...].T
    top[...] = highest


def prob_kernel(slabs, top, *refs):
    scores, keys_t, (outs_t, *probs), grown = refs[:slabs], refs[slabs : 2 * slabs], refs[2 * slabs : -1], refs[-1]
    norm = jnp.zeros(top.shape, F32)
    for slab in range(slabs):
        grown[slab] = jnp.exp(scores[slab][...] - top[...])
        norm = norm + jnp.sum(grown[slab], axis=0, keepdims=True)
    inverse = 1.0 / norm
    for slab in range(slabs):
        probs[slab][...] = (grown[slab] * inverse).astype(BF16)
        part = dot(keys_t[slab][:LATENT, :], probs[slab][...])
        if slab == 0:
            outs_t[...] = part
        else:
            outs_t[...] += part


def out_kernel(heads, index, w_out, w_uv, outs_t, *refs):
    resid, (latents, latents_t, delta, grad_out) = refs[:-4], refs[-4:]
    slabs, rows = len(resid), resid[0].shape[0]
    tok = rows * slabs
    for slab in range(slabs):
        place = lax.rem(index[0] + (slabs - slab), jnp.int32(slabs))
        grad_out[pl.ds(pl.multiple_of(place * rows, rows), rows), :] = dot_last(
            resid[slab][...], w_out[...]
        ).astype(BF16)
    for head in range(heads):
        here = pl.ds(head * tok, tok)
        latents[here, :] = dot(
            grad_out[:, head * VDIM : (head + 1) * VDIM], w_uv[head * VDIM : (head + 1) * VDIM, :]
        ).astype(BF16)
        latents_t[:, here] = latents[here, :].T
    delta[...] = jnp.sum(outs_t[...] * latents_t[...].astype(F32), axis=0, keepdims=True)


def key_kernel(slabs, scale, queries, latents, latents_t, delta, *refs):
    keys, probs, refs = refs[:slabs], refs[slabs : 2 * slabs], refs[2 * slabs :]
    grads, terms = refs[:slabs], refs[slabs:]
    key_count, key_width = keys[0].shape
    share = key_count // len(terms)
    pieces, _, rows, _ = terms[0].shape
    for slab in range(slabs):
        grad_probs = dot(keys[slab][:, :LATENT], latents_t[...])
        grads[slab][...] = (
            scale * probs[slab][...].astype(F32) * (grad_probs - delta[...])
        ).astype(BF16)
        term = dot(grads[slab][...], queries[...])
        term_latent = term[:, :LATENT] + dot(probs[slab][...], latents[...])
        for block, out in enumerate(terms):
            part = slice(block * share, (block + 1) * share)
            out[:, slab, :, :LATENT] = term_latent[part].astype(BF16).reshape(pieces, rows, LATENT)
            out[:, slab, :, LATENT:] = (
                term[part, LATENT:].astype(BF16).reshape(pieces, rows, key_width - LATENT)
            )


def owner_terms(terms):
    (high, low), rest = wide_levels()
    for level in reversed(rest):
        masks = [0, level[0]] if len(level) == 1 else [0, level[1], level[0], level[0] | level[1]]
        group = len(terms) // len(masks)
        terms = [
            total(
                terms[i], *[across(terms[i + group * j], masks[j]) for j in range(1, len(masks))]
            )
            for i in range(group)
        ]
    own, by_low, by_high, corner = terms[0]
    return total(own, across(by_low, low), across(by_high, high), across(corner, high | low))


def query_kernel(slabs, heads, w_uk, *refs):
    keys_t, grads, (grad_nope, grad_pe) = refs[:slabs], refs[slabs : 2 * slabs], refs[2 * slabs :]
    tok = grad_nope.shape[0]
    summed = dot(keys_t[0][...], grads[0][...])
    for slab in range(1, slabs):
        summed = summed + dot(keys_t[slab][...], grads[slab][...])
    for head in range(heads):
        here = slice(head * tok, (head + 1) * tok)
        grad_latent = summed[:LATENT, here].astype(BF16)
        nope = dot(w_uk[head * NOPE : (head + 1) * NOPE, :], grad_latent)
        grad_nope[:, head * NOPE : (head + 1) * NOPE] = nope.T.astype(BF16)
        grad_pe[:, head * ROPE : (head + 1) * ROPE] = summed[LATENT : LATENT + ROPE, here].T.astype(BF16)


def on_device(
    hidden,
    cotangent,
    routes,
    gates,
    offsets,
    w_gate,
    w_up,
    w_down,
    w_out,
    latent,
    rope_key,
    q_nope,
    q_pe,
    w_uk,
    w_uv,
):
    rows, width = hidden.shape
    tok = q_nope.shape[0]
    heads = q_nope.shape[1] // NOPE
    scale = 1.0 / math.sqrt(NOPE + ROPE)
    wide_size, ring = lax.axis_size("wide"), lax.axis_size("narrow")
    wide_index, ring_index = lax.axis_index("wide"), lax.axis_index("narrow")
    experts = wide_size * ring // 2
    (high, low), rest = wide_levels()
    key_width = LATENT + -(-max(ROPE, 2 * experts) // LANES) * LANES
    shape = jax.ShapeDtypeStruct
    turn = ring_index.astype(jnp.int32).reshape(1)
    (payload,) = call(
        functools.partial(pack_kernel, experts),
        [shape((2, rows, width + key_width - LATENT // 2), BF16)],
        [(turn, SMEM), hidden, cotangent, routes.T, gates.T, latent, rope_key.T],
        0,
        8,
        [pltpu.VMEM((tok, ROPE), BF16)],
    )
    payload = payload.reshape(2 * rows, -1)
    routed, keys = routed_sum(payload, rows, w_gate[0].T, w_up[0].T, w_down[0])
    resid_grad = (cotangent.astype(F32) + routed).astype(BF16)

    order = [0, low, high, high | low]
    for level in rest:
        extra = [0, level[0]] if len(level) == 1 else [0, level[1], level[0], level[0] | level[1]]
        order = [mask ^ more for more in extra for mask in order]
    places = wide_index ^ jnp.array(order, jnp.int32)
    turns = (ring_index - jnp.arange(ring, dtype=jnp.int32)) % ring
    bases = offsets[places][None, :] * tok + turns[:, None] * rows
    query_base = (offsets[wide_index] * tok).reshape(1)

    columns, key_count = heads * tok, keys[0].shape[0]
    work = 2 * key_count * columns * key_width
    row = shape((1, columns), F32)
    queries, top, *made = call(
        functools.partial(score_kernel, heads, scale),
        [shape((columns, key_width), BF16), row]
        + [shape((key_count, columns), F32)] * ring
        + [shape((key_width, key_count), BF16)] * ring,
        [(bases, SMEM), (query_base, SMEM), q_nope, q_pe, w_uk, *keys],
        work * ring,
        32,
        [pltpu.VMEM((key_width, columns), BF16)],
    )
    scores, keys_t = made[:ring], made[ring:]
    pieces = [resid_grad, along(resid_grad)]
    outs_t, *probs = call(
        functools.partial(prob_kernel, ring),
        [shape((LATENT, columns), F32)] + [shape((key_count, columns), BF16)] * ring,
        [top, *scores, *keys_t],
        work * ring,
        32,
        [pltpu.VMEM((ring, key_count, columns), F32)],
    )
    for step in range(2, ring):
        tied = queries if step == 2 else outs_t
        pieces.append(along(after(pieces[-1], tied)))
    latents, latents_t, delta = call(
        functools.partial(out_kernel, heads),
        [shape((columns, LATENT), BF16), shape((LATENT, columns), BF16), row],
        [(turn, SMEM), w_out, w_uv, outs_t, *pieces],
        work // 2,
        20,
        [pltpu.VMEM((tok, heads * VDIM), BF16)],
    )
    count = math.prod(2 ** len(level) for level in rest)
    grads = [None] * ring
    arrived = []
    for slabs in (range(1, ring - 1), (ring - 1, 0)):
        made = call(
            functools.partial(key_kernel, len(slabs), scale),
            [shape((key_count, columns), BF16)] * len(slabs)
            + [shape((4, len(slabs), rows, key_width), BF16)] * count,
            [queries, latents, latents_t, delta, *[keys[i] for i in slabs], *[probs[i] for i in slabs]],
            3 * work * len(slabs),
            24,
        )
        sums = owner_terms(made[len(slabs) :])
        for place, slab in enumerate(slabs):
            grads[slab] = made[place]
            moves = [(i, (i - slab) % ring) for i in range(ring)]
            arrived.append(lax.ppermute(sums[place], "narrow", moves) if slab else sums[place])
    grad_q_nope, grad_q_pe = call(
        functools.partial(query_kernel, ring, heads),
        [shape(q_nope.shape, BF16), shape(q_pe.shape, BF16)],
        [w_uk, *keys_t, *grads],
        work * ring,
        24,
    )
    return (
        resid_grad,
        grad_q_nope,
        grad_q_pe,
        sum(part[:, :LATENT].astype(F32) for part in arrived),
        sum(part[:, LATENT : LATENT + ROPE].astype(F32) for part in arrived),
    )


def solution(mesh):
    return jax.shard_map(
        on_device,
        mesh=mesh,
        in_specs=(
            P(("wide", "narrow"), None),
            P(("wide", "narrow"), None),
            P(("wide", "narrow"), None),
            P(("wide", "narrow"), None),
            P(),
            P(("wide", "narrow"), None, None),
            P(("wide", "narrow"), None, None),
            P(("wide", "narrow"), None, None),
            P("narrow", None),
            P("wide", None),
            P("wide", None),
            P("wide", "narrow"),
            P("wide", "narrow"),
            P("narrow", None),
            P("narrow", None),
        ),
        out_specs=(
            P(("wide", "narrow"), None),
            P("wide", "narrow"),
            P("wide", "narrow"),
            P(("wide", "narrow"), None),
            P(("wide", "narrow"), None),
        ),
        check_vma=False,
    )
```

```python
import functools
import math

import jax
import jax.numpy as jnp
from jax import lax
from jax.experimental import pallas as pl
from jax.experimental.pallas import tpu as pltpu
from jax.sharding import PartitionSpec as P

LATENT = 512
NOPE = 128
ROPE = 64
VDIM = 128

F32 = jnp.float32
BF16 = jnp.bfloat16
CONTRACT_LAST = (((1,), (1,)), ((), ()))


def across(value, mask):
    pairs = [(source, source ^ mask) for source in range(lax.axis_size("wide"))]
    return lax.ppermute(value, "wide", pairs)


def along(value):
    size = lax.axis_size("narrow")
    return lax.ppermute(value, "narrow", [(i, (i + 1) % size) for i in range(size)])


def wide_levels():
    size = lax.axis_size("wide")
    masks = []
    mask = size // 2
    while mask:
        masks.append(mask)
        mask //= 2
    first, rest = masks[:2], masks[2:]
    return first, [rest[i : i + 2] for i in range(0, len(rest), 2)]


def gather_level(block, level):
    if len(level) == 1:
        return [block, across(block, level[0])]
    high, low = level
    by_low, by_high = across(block, low), across(block, high)
    half = block.shape[0] // 2
    corner = jnp.concatenate([across(by_low[:half], high), across(by_high[half:], low)], axis=0)
    return [block, by_low, by_high, corner]


def total(*terms):
    summed = terms[0].astype(F32)
    for term in terms[1:]:
        summed = summed + term.astype(F32)
    return summed.astype(BF16)


def scatter_level(blocks, level):
    if len(level) == 1:
        return total(blocks[0], across(blocks[1], level[0]))
    high, low = level
    own, by_low, by_high, corner = blocks
    half = own.shape[1] // 2
    from_high = across(corner[:, :half], high)
    from_low = across(corner[:, half:], low)
    by_low = jnp.concatenate([total(by_low[:, :half], from_high), by_low[:, half:]], axis=1)
    by_high = jnp.concatenate([by_high[:, :half], total(by_high[:, half:], from_low)], axis=1)
    return total(own, across(by_low, low), across(by_high, high))

LANES = 128
VMEM = pl.BlockSpec(memory_space=pltpu.VMEM)
SMEM = pl.BlockSpec(memory_space=pltpu.SMEM)


def dot(left, right):
    return jnp.dot(left, right, preferred_element_type=F32)


def dot_last(left, right):
    return lax.dot_general(left, right, CONTRACT_LAST, preferred_element_type=F32)


def call(kernel, outs, ins, flops, limit, scratch=()):
    specs = [entry[1] if isinstance(entry, tuple) else VMEM for entry in ins]
    arrays = [entry[0] if isinstance(entry, tuple) else entry for entry in ins]
    moved = sum(math.prod(out.shape) * out.dtype.itemsize for out in outs)
    moved += sum(array.size * array.dtype.itemsize for array in arrays)
    return pl.pallas_call(
        kernel,
        out_shape=outs,
        in_specs=specs,
        out_specs=[VMEM] * len(outs),
        scratch_shapes=list(scratch),
        compiler_params=pltpu.CompilerParams(vmem_limit_bytes=limit * 2**20),
        cost_estimate=pl.CostEstimate(flops=flops, bytes_accessed=moved, transcendentals=0),
    )(*arrays)


def pack_kernel(experts, index, hidden, cotangent, routes, gates, latent, rope, out, turned):
    rows, width = hidden.shape
    half = latent.shape[1] // 2
    tail = out.shape[2] - width - half
    place = pl.ds(pl.multiple_of(index[0] * rows, rows), rows)
    out[0, :, :width] = hidden[...]
    out[1, :, :width] = cotangent[...]
    out[0, :, width : width + half] = latent[place, :half]
    out[1, :, width : width + half] = latent[place, half:]
    turned[...] = rope[...].T
    out[0, :, width + half :] = jnp.zeros((rows, tail), BF16)
    out[0, :, width + half : width + half + ROPE] = turned[place, :]
    line = lax.broadcasted_iota(jnp.int32, (tail, rows), 0)
    first = jnp.zeros((tail, rows), F32)
    second = jnp.zeros((tail, rows), F32)
    for k in range(routes.shape[0]):
        chosen, weight = routes[k : k + 1, :], gates[k : k + 1, :]
        first = first + jnp.where(line == chosen, weight, 0.0)
        second = second + jnp.where(line == chosen + experts, weight, 0.0)
    second = second - second.astype(BF16).astype(F32)
    out[1, :, width + half :] = (first + second).T.astype(BF16)


def expert_kernel(experts, expert_ref, tokens, w_both, w_down, keys, out):
    pieces, _, rows, wide = tokens.shape
    hidden_units, width = w_down.shape
    merged = pieces * rows
    tail = keys.shape[1] - LATENT
    half = wide - tail
    x_rows = tokens[:, 0, :, :width].reshape(merged, width)
    dy_rows = tokens[:, 1, :, :width].reshape(merged, width)
    keys[:, : half - width] = tokens[:, 0, :, width:half].reshape(merged, half - width)
    keys[:, half - width : LATENT] = tokens[:, 1, :, width:half].reshape(merged, half - width)
    keys[:, LATENT:] = tokens[:, 0, :, half:].reshape(merged, tail)
    parts = tokens[:, 1, :, half:].reshape(merged, tail).astype(F32)
    lane = lax.broadcasted_iota(jnp.int32, (merged, tail), 1)
    mine = (lane == expert_ref[0]) | (lane == expert_ref[0] + experts)
    gate = jnp.sum(jnp.where(mine, parts, 0.0), axis=1, keepdims=True)
    pre_gate = dot_last(x_rows, w_both[:hidden_units, :])
    up_value = dot_last(x_rows, w_both[hidden_units:, :])
    grad_hidden = gate * dot_last(dy_rows, w_down[...])
    sigmoid_gate = jax.nn.sigmoid(pre_gate)
    scaled = grad_hidden * sigmoid_gate
    grad_gate = scaled * up_value * (1.0 + pre_gate * (1.0 - sigmoid_gate))
    grad_up = scaled * pre_gate
    both = jnp.concatenate([grad_gate.astype(BF16), grad_up.astype(BF16)], axis=1)
    out[...] = dot(both, w_both[...]).astype(BF16)


def after(value, *earlier):
    return lax.optimization_barrier((value, *earlier))[0]


def routed_sum(payload, rows, w_gate, w_up, w_down):
    wide_size, ring = lax.axis_size("wide"), lax.axis_size("narrow")
    wide_index, ring_index = lax.axis_index("wide"), lax.axis_index("narrow")
    experts = wide_size * ring // 2
    expert = ((wide_index * ring + ring_index) // 2).astype(jnp.int32).reshape(1)
    wide, width = payload.shape[1], w_down.shape[1]
    (high, low), rest = wide_levels()
    w_both = jnp.concatenate([w_gate, w_up], axis=0)
    key_width = LATENT + wide - width - LATENT // 2

    def experts_of(block):
        return call(
            functools.partial(expert_kernel, experts),
            [jax.ShapeDtypeStruct((4 * rows, key_width), BF16), jax.ShapeDtypeStruct((4 * rows, width), BF16)],
            [(expert, SMEM), block.reshape(4, 2, rows, wide), w_both, w_down],
            40 * rows * w_both.size // 2,
            18,
        )

    def spread(block):
        blocks = [block]
        for level in rest:
            blocks = [piece for one in zip(*[gather_level(b, level) for b in blocks]) for piece in one]
        return blocks

    def collect(sums):
        for level in reversed(rest):
            group = len(sums) // 2 ** len(level)
            sums = [
                scatter_level([sums[i + group * j] for j in range(2 ** len(level))], level)
                for i in range(group)
            ]
        return sums[0]

    columns, sides, slabs, results, sums = [payload], [], [], [], []
    for turn in range(ring + 1):
        moving, beside = [], []
        if turn > 0:
            by_low, by_high = sides[turn - 1]
            moving += [across(by_low[:rows], high), across(by_high[rows:], low)]
        if turn < ring:
            moving += [across(columns[turn], low), across(columns[turn], high)]
        if turn < ring - 1:
            moving.append(along(columns[turn]))
        if turn > 1:
            blocks = spread(slabs[turn - 2])
            results.append([experts_of(block) for block in blocks])
            beside += [result[1] for result in results[-1]][: None if turn < ring else 1]
        if turn > 2:
            sums.append(collect([result[1] for result in results[turn - 3]]))
            beside.append(sums[-1])
        moving = list(lax.optimization_barrier((*moving, *beside)))[: len(moving)]
        if turn < ring - 1:
            columns.append(moving.pop())
        if turn < ring:
            sides.append(moving[-2:])
        if turn > 0:
            parts = [columns[turn - 1], *sides[turn - 1], *moving[:2]]
            slabs.append(jnp.concatenate(parts, axis=0))
    def parts_of(step):
        return list(sums[step].reshape(4, rows, width))

    def sides_of(step):
        _, by_low, by_high, _ = parts_of(step)
        return [across(by_low, low), across(by_high, high)]

    def together(*values):
        return list(lax.optimization_barrier(values))

    last = ring - 1
    link = corner = None
    for step in range(1, last - 1):
        moving = sides_of(step) + [along(total(parts_of(step)[3], *([] if corner is None else [corner])))]
        if link is not None:
            moving.append(along(link))
        beside = []
        if step == last - 2:
            first, *others = spread(slabs[last])
            sums.append(collect([result[1] for result in results[last - 1]]))
            others = [experts_of(after(block, *[r[1] for r in results[last - 1]])) for block in others]
            first = experts_of(after(first, sums[last - 1], *[result[1] for result in others]))
            results.append([first, *others])
            sums.append(collect([result[1] for result in results[last]]))
            beside = [sums[last - 1], first[1], sums[last]]
        moving = together(*moving, *beside)[: len(moving)]
        corner = moving[2]
        link = total(parts_of(step)[0], *moving[:2], *moving[3:])
    own, _, _, far = parts_of(last - 1)
    moving = together(
        *sides_of(last - 1), along(total(far, corner)), along(link), *sides_of(last)
    )
    link = total(own, *moving[:2], moving[3])
    own, _, _, far = parts_of(last)
    far = total(far, moving[2])
    ends = moving[4:]
    home = [parts_of(0)[0], *sides_of(0), across(parts_of(0)[3], high | low)]
    moving = together(across(far, high | low), along(link))
    link = total(own, *ends, *moving)
    home = total(*home)
    keys = [result[0] for slab in results for result in slab]
    return home.astype(F32) + along(link).astype(F32), keys


def score_kernel(heads, scale, bases, query_base, q_nope, q_pe, w_uk, *refs):
    slabs, pieces = bases.shape
    keys, (queries, top, *rest), queries_t = refs[:slabs], refs[slabs:-1], refs[-1]
    scores, keys_t = rest[:slabs], rest[slabs:]
    tok = q_nope.shape[0]
    key_count, key_width = keys[0].shape
    columns = heads * tok
    rows = key_count // pieces
    queries[:, LATENT:] = jnp.zeros((columns, key_width - LATENT), BF16)
    for head in range(heads):
        here = pl.ds(head * tok, tok)
        queries[here, :LATENT] = dot(
            q_nope[:, head * NOPE : (head + 1) * NOPE], w_uk[head * NOPE : (head + 1) * NOPE, :]
        ).astype(BF16)
        queries[here, LATENT : LATENT + ROPE] = q_pe[:, head * ROPE : (head + 1) * ROPE]
        queries_t[:, here] = queries[here, :].T
    position = query_base[0] + lax.rem(
        lax.broadcasted_iota(jnp.int32, (rows, columns), 1), jnp.int32(tok)
    )
    ahead = lax.broadcasted_iota(jnp.int32, (rows, columns), 0) - position
    highest = jnp.full((1, columns), -1e30, F32)
    for slab in range(slabs):
        raw = dot(keys[slab][...], queries_t[...])
        for piece in range(pieces):
            here = slice(piece * rows, (piece + 1) * rows)
            shown = ahead + bases[slab, piece] <= 0
            masked = jnp.where(shown, raw[here, :] * scale, -1e30)
            scores[slab][here, :] = masked
            highest = jnp.maximum(highest, jnp.max(masked, axis=0, keepdims=True))
        keys_t[slab][...] = keys[slab][...].T
    top[...] = highest


def prob_kernel(slabs, top, *refs):
    scores, keys_t, (outs_t, *probs), grown = refs[:slabs], refs[slabs : 2 * slabs], refs[2 * slabs : -1], refs[-1]
    norm = jnp.zeros(top.shape, F32)
    for slab in range(slabs):
        grown[slab] = jnp.exp(scores[slab][...] - top[...])
        norm = norm + jnp.sum(grown[slab], axis=0, keepdims=True)
    inverse = 1.0 / norm
    for slab in range(slabs):
        probs[slab][...] = (grown[slab] * inverse).astype(BF16)
        part = dot(keys_t[slab][:LATENT, :], probs[slab][...])
        if slab == 0:
            outs_t[...] = part
        else:
            outs_t[...] += part


def out_kernel(heads, index, w_out, w_uv, outs_t, *refs):
    resid, (latents, latents_t, delta, grad_out) = refs[:-4], refs[-4:]
    slabs, rows = len(resid), resid[0].shape[0]
    tok = rows * slabs
    for slab in range(slabs):
        place = lax.rem(index[0] + (slabs - slab), jnp.int32(slabs))
        grad_out[pl.ds(pl.multiple_of(place * rows, rows), rows), :] = dot_last(
            resid[slab][...], w_out[...]
        ).astype(BF16)
    for head in range(heads):
        here = pl.ds(head * tok, tok)
        latents[here, :] = dot(
            grad_out[:, head * VDIM : (head + 1) * VDIM], w_uv[head * VDIM : (head + 1) * VDIM, :]
        ).astype(BF16)
        latents_t[:, here] = latents[here, :].T
    delta[...] = jnp.sum(outs_t[...] * latents_t[...].astype(F32), axis=0, keepdims=True)


def key_kernel(slabs, scale, queries, latents, latents_t, delta, *refs):
    keys, probs, refs = refs[:slabs], refs[slabs : 2 * slabs], refs[2 * slabs :]
    grads, terms = refs[:slabs], refs[slabs:]
    key_count, key_width = keys[0].shape
    pieces, _, rows, _ = terms[0].shape
    for slab in range(slabs):
        grad_probs = dot(keys[slab][:, :LATENT], latents_t[...])
        grads[slab][...] = (
            scale * probs[slab][...].astype(F32) * (grad_probs - delta[...])
        ).astype(BF16)
        term = dot(grads[slab][...], queries[...])
        term_latent = term[:, :LATENT] + dot(probs[slab][...], latents[...])
        out, place = terms[slab % len(terms)], slab // len(terms)
        out[:, place, :, :LATENT] = term_latent.astype(BF16).reshape(pieces, rows, LATENT)
        out[:, place, :, LATENT:] = (
            term[:, LATENT:].astype(BF16).reshape(pieces, rows, key_width - LATENT)
        )


def owner_terms(terms):
    (high, low), rest = wide_levels()
    for level in reversed(rest):
        masks = [0, level[0]] if len(level) == 1 else [0, level[1], level[0], level[0] | level[1]]
        group = len(terms) // len(masks)
        terms = [
            total(
                terms[i], *[across(terms[i + group * j], masks[j]) for j in range(1, len(masks))]
            )
            for i in range(group)
        ]
    own, by_low, by_high, corner = terms[0]
    return total(own, across(by_low, low), across(by_high, high), across(corner, high | low))


def query_kernel(slabs, heads, w_uk, *refs):
    keys_t, grads, (grad_nope, grad_pe) = refs[:slabs], refs[slabs : 2 * slabs], refs[2 * slabs :]
    tok = grad_nope.shape[0]
    summed = dot(keys_t[0][...], grads[0][...])
    for slab in range(1, slabs):
        summed = summed + dot(keys_t[slab][...], grads[slab][...])
    for head in range(heads):
        here = slice(head * tok, (head + 1) * tok)
        grad_latent = summed[:LATENT, here].astype(BF16)
        nope = dot(w_uk[head * NOPE : (head + 1) * NOPE, :], grad_latent)
        grad_nope[:, head * NOPE : (head + 1) * NOPE] = nope.T.astype(BF16)
        grad_pe[:, head * ROPE : (head + 1) * ROPE] = summed[LATENT : LATENT + ROPE, here].T.astype(BF16)


def on_device(
    hidden,
    cotangent,
    routes,
    gates,
    offsets,
    w_gate,
    w_up,
    w_down,
    w_out,
    latent,
    rope_key,
    q_nope,
    q_pe,
    w_uk,
    w_uv,
):
    rows, width = hidden.shape
    tok = q_nope.shape[0]
    heads = q_nope.shape[1] // NOPE
    scale = 1.0 / math.sqrt(NOPE + ROPE)
    wide_size, ring = lax.axis_size("wide"), lax.axis_size("narrow")
    wide_index, ring_index = lax.axis_index("wide"), lax.axis_index("narrow")
    experts = wide_size * ring // 2
    (high, low), rest = wide_levels()
    key_width = LATENT + -(-max(ROPE, 2 * experts) // LANES) * LANES
    shape = jax.ShapeDtypeStruct
    turn = ring_index.astype(jnp.int32).reshape(1)
    (payload,) = call(
        functools.partial(pack_kernel, experts),
        [shape((2, rows, width + key_width - LATENT // 2), BF16)],
        [(turn, SMEM), hidden, cotangent, routes.T, gates.T, latent, rope_key.T],
        0,
        8,
        [pltpu.VMEM((tok, ROPE), BF16)],
    )
    payload = payload.reshape(2 * rows, -1)
    routed, keys = routed_sum(payload, rows, w_gate[0].T, w_up[0].T, w_down[0])
    resid_grad = (cotangent.astype(F32) + routed).astype(BF16)

    order = [0, low, high, high | low]
    for level in rest:
        extra = [0, level[0]] if len(level) == 1 else [0, level[1], level[0], level[0] | level[1]]
        order = [mask ^ more for more in extra for mask in order]
    places = wide_index ^ jnp.array(order, jnp.int32)
    turns = (ring_index - jnp.arange(ring, dtype=jnp.int32)) % ring
    bases = (offsets[places][None, :] * tok + turns[:, None] * rows).reshape(len(keys), 4)
    query_base = (offsets[wide_index] * tok).reshape(1)

    columns, key_count, groups = heads * tok, keys[0].shape[0], len(keys)
    work = 2 * key_count * columns * key_width
    row = shape((1, columns), F32)
    queries, top, *made = call(
        functools.partial(score_kernel, heads, scale),
        [shape((columns, key_width), BF16), row]
        + [shape((key_count, columns), F32)] * groups
        + [shape((key_width, key_count), BF16)] * groups,
        [(bases, SMEM), (query_base, SMEM), q_nope, q_pe, w_uk, *keys],
        work * groups,
        32,
        [pltpu.VMEM((key_width, columns), BF16)],
    )
    scores, keys_t = made[:groups], made[groups:]
    pieces = [resid_grad, along(resid_grad)]
    outs_t, *probs = call(
        functools.partial(prob_kernel, groups),
        [shape((LATENT, columns), F32)] + [shape((key_count, columns), BF16)] * groups,
        [top, *scores, *keys_t],
        work * groups,
        32,
        [pltpu.VMEM((groups, key_count, columns), F32)],
    )
    for step in range(2, ring):
        tied = queries if step == 2 else outs_t
        pieces.append(along(after(pieces[-1], tied)))
    latents, latents_t, delta = call(
        functools.partial(out_kernel, heads),
        [shape((columns, LATENT), BF16), shape((LATENT, columns), BF16), row],
        [(turn, SMEM), w_out, w_uv, outs_t, *pieces],
        work,
        20,
        [pltpu.VMEM((tok, heads * VDIM), BF16)],
    )
    count = groups // ring
    grads = [None] * groups
    arrived = []
    for slabs in (range(1, ring - 1), (ring - 1, 0)):
        chosen = [slab * count + block for slab in slabs for block in range(count)]
        made = call(
            functools.partial(key_kernel, len(chosen), scale),
            [shape((key_count, columns), BF16)] * len(chosen)
            + [shape((4, len(slabs), rows, key_width), BF16)] * count,
            [queries, latents, latents_t, delta, *[keys[i] for i in chosen], *[probs[i] for i in chosen]],
            3 * work * len(chosen),
            24,
        )
        for place, group in enumerate(chosen):
            grads[group] = made[place]
        sums = owner_terms(made[len(chosen) :])
        for place, slab in enumerate(slabs):
            moves = [(i, (i - slab) % ring) for i in range(ring)]
            arrived.append(lax.ppermute(sums[place], "narrow", moves) if slab else sums[place])
    grad_q_nope, grad_q_pe = call(
        functools.partial(query_kernel, groups, heads),
        [shape(q_nope.shape, BF16), shape(q_pe.shape, BF16)],
        [w_uk, *keys_t, *grads],
        work * groups,
        24,
    )
    return (
        resid_grad,
        grad_q_nope,
        grad_q_pe,
        sum(part[:, :LATENT].astype(F32) for part in arrived),
        sum(part[:, LATENT : LATENT + ROPE].astype(F32) for part in arrived),
    )


def solution(mesh):
    return jax.shard_map(
        on_device,
        mesh=mesh,
        in_specs=(
            P(("wide", "narrow"), None),
            P(("wide", "narrow"), None),
            P(("wide", "narrow"), None),
            P(("wide", "narrow"), None),
            P(),
            P(("wide", "narrow"), None, None),
            P(("wide", "narrow"), None, None),
            P(("wide", "narrow"), None, None),
            P("narrow", None),
            P("wide", None),
            P("wide", None),
            P("wide", "narrow"),
            P("wide", "narrow"),
            P("narrow", None),
            P("narrow", None),
        ),
        out_specs=(
            P(("wide", "narrow"), None),
            P("wide", "narrow"),
            P("wide", "narrow"),
            P(("wide", "narrow"), None),
            P(("wide", "narrow"), None),
        ),
        check_vma=False,
    )
```

```python
import functools
import math

import jax
import jax.numpy as jnp
from jax import lax
from jax.experimental import pallas as pl
from jax.experimental.pallas import tpu as pltpu
from jax.sharding import PartitionSpec as P

LATENT = 512
NOPE = 128
ROPE = 64
VDIM = 128

F32 = jnp.float32
BF16 = jnp.bfloat16
CONTRACT_LAST = (((1,), (1,)), ((), ()))


def across(value, mask):
    pairs = [(source, source ^ mask) for source in range(lax.axis_size("wide"))]
    return lax.ppermute(value, "wide", pairs)


def along(value):
    size = lax.axis_size("narrow")
    return lax.ppermute(value, "narrow", [(i, (i + 1) % size) for i in range(size)])


def wide_levels():
    size = lax.axis_size("wide")
    masks = []
    mask = size // 2
    while mask:
        masks.append(mask)
        mask //= 2
    first, rest = masks[:2], masks[2:]
    return first, [rest[i : i + 2] for i in range(0, len(rest), 2)]


def gather_level(block, level):
    if len(level) == 1:
        return [block, across(block, level[0])]
    high, low = level
    by_low, by_high = across(block, low), across(block, high)
    half = block.shape[0] // 2
    corner = jnp.concatenate([across(by_low[:half], high), across(by_high[half:], low)], axis=0)
    return [block, by_low, by_high, corner]


def total(*terms):
    summed = terms[0].astype(F32)
    for term in terms[1:]:
        summed = summed + term.astype(F32)
    return summed.astype(BF16)


def scatter_level(blocks, level):
    if len(level) == 1:
        return total(blocks[0], across(blocks[1], level[0]))
    high, low = level
    own, by_low, by_high, corner = blocks
    half = own.shape[1] // 2
    from_high = across(corner[:, :half], high)
    from_low = across(corner[:, half:], low)
    by_low = jnp.concatenate([total(by_low[:, :half], from_high), by_low[:, half:]], axis=1)
    by_high = jnp.concatenate([by_high[:, :half], total(by_high[:, half:], from_low)], axis=1)
    return total(own, across(by_low, low), across(by_high, high))

LANES = 128
PACK_LIMIT = 56
VMEM = pl.BlockSpec(memory_space=pltpu.VMEM)
SMEM = pl.BlockSpec(memory_space=pltpu.SMEM)
HBM = pl.BlockSpec(memory_space=pltpu.HBM)


def dot(left, right):
    return jnp.dot(left, right, preferred_element_type=F32)


def dot_last(left, right):
    return lax.dot_general(left, right, CONTRACT_LAST, preferred_element_type=F32)


def call(kernel, outs, ins, flops, limit, scratch=()):
    specs = [entry[1] if isinstance(entry, tuple) else VMEM for entry in ins]
    arrays = [entry[0] if isinstance(entry, tuple) else entry for entry in ins]
    moved = sum(math.prod(out.shape) * out.dtype.itemsize for out in outs)
    moved += sum(array.size * array.dtype.itemsize for array in arrays)
    return pl.pallas_call(
        kernel,
        out_shape=outs,
        in_specs=specs,
        out_specs=[VMEM] * len(outs),
        scratch_shapes=list(scratch),
        compiler_params=pltpu.CompilerParams(vmem_limit_bytes=limit * 2**20),
        cost_estimate=pl.CostEstimate(flops=flops, bytes_accessed=moved, transcendentals=0),
    )(*arrays)


def pack_kernel(experts, index, hidden, cotangent, routes, gates, latent, rope, out, *scratch):
    *held, turned, sems = scratch
    rows, width = hidden.shape
    half = latent.shape[1] // 2
    tail = out.shape[2] - width - half
    place = pl.ds(pl.multiple_of(index[0] * rows, rows), rows)
    sources = [rope, routes, gates, latent.at[place, :], hidden, cotangent]
    copies = [
        pltpu.make_async_copy(source, target, sems.at[i])
        for i, (source, target) in enumerate(zip(sources, held))
    ]
    for copy in copies:
        copy.start()
    for copy in copies[:3]:
        copy.wait()
    rope_held, routes_held, gates_held, latent_held, hidden_held, cotangent_held = held
    turned[...] = rope_held[...].T
    out[0, :, width + half :] = jnp.zeros((rows, tail), BF16)
    out[0, :, width + half : width + half + ROPE] = turned[place, :]
    line = lax.broadcasted_iota(jnp.int32, (tail, rows), 0)
    first = jnp.zeros((tail, rows), F32)
    second = jnp.zeros((tail, rows), F32)
    for k in range(routes.shape[0]):
        chosen, weight = routes_held[k : k + 1, :], gates_held[k : k + 1, :]
        first = first + jnp.where(line == chosen, weight, 0.0)
        second = second + jnp.where(line == chosen + experts, weight, 0.0)
    second = second - second.astype(BF16).astype(F32)
    out[1, :, width + half :] = (first + second).T.astype(BF16)
    for copy in copies[3:]:
        copy.wait()
    out[0, :, width : width + half] = latent_held[:, :half]
    out[1, :, width : width + half] = latent_held[:, half:]
    out[0, :, :width] = hidden_held[...]
    out[1, :, :width] = cotangent_held[...]


def expert_kernel(experts, expert_ref, tokens, w_both, w_down, keys, out):
    pieces, _, rows, wide = tokens.shape
    hidden_units, width = w_down.shape
    merged = pieces * rows
    tail = keys.shape[1] - LATENT
    half = wide - tail
    x_rows = tokens[:, 0, :, :width].reshape(merged, width)
    dy_rows = tokens[:, 1, :, :width].reshape(merged, width)
    keys[:, : half - width] = tokens[:, 0, :, width:half].reshape(merged, half - width)
    keys[:, half - width : LATENT] = tokens[:, 1, :, width:half].reshape(merged, half - width)
    keys[:, LATENT:] = tokens[:, 0, :, half:].reshape(merged, tail)
    parts = tokens[:, 1, :, half:].reshape(merged, tail).astype(F32)
    lane = lax.broadcasted_iota(jnp.int32, (merged, tail), 1)
    mine = (lane == expert_ref[0]) | (lane == expert_ref[0] + experts)
    gate = jnp.sum(jnp.where(mine, parts, 0.0), axis=1, keepdims=True)
    pre_gate = dot_last(x_rows, w_both[:hidden_units, :])
    up_value = dot_last(x_rows, w_both[hidden_units:, :])
    grad_hidden = gate * dot_last(dy_rows, w_down[...])
    sigmoid_gate = jax.nn.sigmoid(pre_gate)
    scaled = grad_hidden * sigmoid_gate
    grad_gate = scaled * up_value * (1.0 + pre_gate * (1.0 - sigmoid_gate))
    grad_up = scaled * pre_gate
    both = jnp.concatenate([grad_gate.astype(BF16), grad_up.astype(BF16)], axis=1)
    out[...] = dot(both, w_both[...]).astype(BF16)


def after(value, *earlier):
    return lax.optimization_barrier((value, *earlier))[0]


def routed_sum(payload, rows, w_gate, w_up, w_down):
    wide_size, ring = lax.axis_size("wide"), lax.axis_size("narrow")
    wide_index, ring_index = lax.axis_index("wide"), lax.axis_index("narrow")
    experts = wide_size * ring // 2
    expert = ((wide_index * ring + ring_index) // 2).astype(jnp.int32).reshape(1)
    wide, width = payload.shape[1], w_down.shape[1]
    (high, low), rest = wide_levels()
    w_both = jnp.concatenate([w_gate, w_up], axis=0)
    key_width = LATENT + wide - width - LATENT // 2

    def experts_of(block):
        return call(
            functools.partial(expert_kernel, experts),
            [jax.ShapeDtypeStruct((4 * rows, key_width), BF16), jax.ShapeDtypeStruct((4 * rows, width), BF16)],
            [(expert, SMEM), block.reshape(4, 2, rows, wide), w_both, w_down],
            40 * rows * w_both.size // 2,
            18,
        )

    def spread(block):
        blocks = [block]
        for level in rest:
            blocks = [piece for one in zip(*[gather_level(b, level) for b in blocks]) for piece in one]
        return blocks

    def collect(sums):
        for level in reversed(rest):
            group = len(sums) // 2 ** len(level)
            sums = [
                scatter_level([sums[i + group * j] for j in range(2 ** len(level))], level)
                for i in range(group)
            ]
        return sums[0]

    def together(*values):
        return list(lax.optimization_barrier(values))

    def with_room(column):
        return jnp.concatenate([column, column[:rows]], axis=0)

    def filled(room, half):
        return lax.dynamic_update_slice_in_dim(room, half, 2 * rows, 0)

    slabs, results, sums = [], [], []
    column, rooms, sides, former = payload, None, None, None
    for turn in range(ring + 1):
        if turn == 0:
            moving = [across(column, low), across(column, high), along(column)]
            beside = [w_both]
        else:
            halves = [sides[1][rows:], sides[0][:rows]]
            sent = [filled(*pair) for pair in zip(rooms, halves)] if turn < ring else halves
            moving = [across(sent[0], low), across(sent[1], high)]
            if turn < ring - 1:
                moving.append(along(column))
            beside = []
        if turn > 1:
            blocks = spread(after(slabs[turn - 2], *sent))
            results.append([experts_of(block) for block in blocks])
            beside += [result[1] for result in results[-1]][: None if turn < ring else 1]
        if turn > 2:
            sums.append(collect([result[1] for result in results[turn - 3]]))
            beside.append(sums[-1])
        if turn < ring - 1:
            beside += [with_room(moving[2]), with_room(moving[2])]
        done = together(*moving, *beside)
        if turn > 0:
            corner = [part[-rows:] for part in done[:2]]
            slabs.append(jnp.concatenate([former, *sides, corner[1], corner[0]], axis=0))
        if turn == 0:
            w_both = done[3]
        if turn < ring:
            sides = [part[: 2 * rows] for part in done[:2]]
        former = column
        if turn < ring - 1:
            column, rooms = done[2], done[-2:]

    def parts_of(step):
        return list(sums[step].reshape(4, rows, width))

    last = ring - 1
    link = corner = None
    for step in range(1, last - 1):
        own, by_low, by_high, far = parts_of(step)
        moving = [
            across(by_low, low),
            across(by_high, high),
            along(far if corner is None else total(far, corner)),
        ]
        if link is not None:
            moving.append(along(link))
        count, beside = len(moving), []
        if step == last - 2:
            first, *others = spread(slabs[last])
            before = [result[1] for result in results[last - 1]]
            beside = [*before[1:], *others]
        done = together(*moving, *beside)
        corner = done[2]
        link = total(own, *done[:2], *done[3:count])
    others = [experts_of(block) for block in done[-len(others) :]]
    sums.append(collect(before))
    home, home_low, home_high, home_far = parts_of(0)
    link, home_far, sums[last - 1], *_ = together(
        along(link), across(home_far, high | low), sums[last - 1], *[result[1] for result in others]
    )
    own, by_low, by_high, far = parts_of(last - 1)
    first = experts_of(after(first, home_far))
    results.append([first, *others])
    sums.append(collect([result[1] for result in results[last]]))
    by_low, by_high, corner, sums[last] = together(
        across(by_low, low), across(by_high, high), along(total(far, corner)), sums[last]
    )
    link = total(own, by_low, by_high, link)
    own, by_low, by_high, far = parts_of(last)
    done = together(
        across(by_low, low), across(by_high, high), across(total(far, corner), high | low), along(link)
    )
    link = total(own, *done)
    home = total(home, home_far, across(home_low, low), across(home_high, high))
    keys = [result[0] for slab in results for result in slab]
    return home.astype(F32) + along(link).astype(F32), keys


def score_kernel(heads, scale, bases, query_base, q_nope, q_pe, w_uk, *refs):
    slabs, pieces = bases.shape
    keys, (queries, top, *rest), queries_t = refs[:slabs], refs[slabs:-1], refs[-1]
    scores, keys_t = rest[:slabs], rest[slabs:]
    tok = q_nope.shape[0]
    key_count, key_width = keys[0].shape
    columns = heads * tok
    rows = key_count // pieces
    queries[:, LATENT:] = jnp.zeros((columns, key_width - LATENT), BF16)
    for head in range(heads):
        here = pl.ds(head * tok, tok)
        queries[here, :LATENT] = dot(
            q_nope[:, head * NOPE : (head + 1) * NOPE], w_uk[head * NOPE : (head + 1) * NOPE, :]
        ).astype(BF16)
        queries[here, LATENT : LATENT + ROPE] = q_pe[:, head * ROPE : (head + 1) * ROPE]
        queries_t[:, here] = queries[here, :].T
    position = query_base[0] + lax.rem(
        lax.broadcasted_iota(jnp.int32, (rows, columns), 1), jnp.int32(tok)
    )
    ahead = lax.broadcasted_iota(jnp.int32, (rows, columns), 0) - position
    highest = jnp.full((1, columns), -1e30, F32)
    for slab in range(slabs):
        raw = dot(keys[slab][...], queries_t[...])
        for piece in range(pieces):
            here = slice(piece * rows, (piece + 1) * rows)
            shown = ahead + bases[slab, piece] <= 0
            masked = jnp.where(shown, raw[here, :] * scale, -1e30)
            scores[slab][here, :] = masked
            highest = jnp.maximum(highest, jnp.max(masked, axis=0, keepdims=True))
        keys_t[slab][...] = keys[slab][...].T
    top[...] = highest


def prob_kernel(slabs, top, *refs):
    scores, keys_t, (outs_t, *probs), grown = refs[:slabs], refs[slabs : 2 * slabs], refs[2 * slabs : -1], refs[-1]
    norm = jnp.zeros(top.shape, F32)
    for slab in range(slabs):
        grown[slab] = jnp.exp(scores[slab][...] - top[...])
        norm = norm + jnp.sum(grown[slab], axis=0, keepdims=True)
    inverse = 1.0 / norm
    for slab in range(slabs):
        probs[slab][...] = (grown[slab] * inverse).astype(BF16)
        part = dot(keys_t[slab][:LATENT, :], probs[slab][...])
        if slab == 0:
            outs_t[...] = part
        else:
            outs_t[...] += part


def out_kernel(heads, index, w_out, w_uv, outs_t, *refs):
    resid, (latents, latents_t, delta, grad_out) = refs[:-4], refs[-4:]
    slabs, rows = len(resid), resid[0].shape[0]
    tok = rows * slabs
    for slab in range(slabs):
        place = lax.rem(index[0] + (slabs - slab), jnp.int32(slabs))
        grad_out[pl.ds(pl.multiple_of(place * rows, rows), rows), :] = dot_last(
            resid[slab][...], w_out[...]
        ).astype(BF16)
    for head in range(heads):
        here = pl.ds(head * tok, tok)
        latents[here, :] = dot(
            grad_out[:, head * VDIM : (head + 1) * VDIM], w_uv[head * VDIM : (head + 1) * VDIM, :]
        ).astype(BF16)
        latents_t[:, here] = latents[here, :].T
    delta[...] = jnp.sum(outs_t[...] * latents_t[...].astype(F32), axis=0, keepdims=True)


def key_kernel(slabs, scale, queries, latents, latents_t, delta, *refs):
    keys, probs, refs = refs[:slabs], refs[slabs : 2 * slabs], refs[2 * slabs :]
    grads, terms = refs[:slabs], refs[slabs:]
    key_count, key_width = keys[0].shape
    pieces, _, rows, _ = terms[0].shape
    for slab in range(slabs):
        grad_probs = dot(keys[slab][:, :LATENT], latents_t[...])
        grads[slab][...] = (
            scale * probs[slab][...].astype(F32) * (grad_probs - delta[...])
        ).astype(BF16)
        term = dot(grads[slab][...], queries[...])
        term_latent = term[:, :LATENT] + dot(probs[slab][...], latents[...])
        out, place = terms[slab % len(terms)], slab // len(terms)
        out[:, place, :, :LATENT] = term_latent.astype(BF16).reshape(pieces, rows, LATENT)
        out[:, place, :, LATENT:] = (
            term[:, LATENT:].astype(BF16).reshape(pieces, rows, key_width - LATENT)
        )


def owner_terms(terms):
    (high, low), rest = wide_levels()
    for level in reversed(rest):
        masks = [0, level[0]] if len(level) == 1 else [0, level[1], level[0], level[0] | level[1]]
        group = len(terms) // len(masks)
        terms = [
            total(
                terms[i], *[across(terms[i + group * j], masks[j]) for j in range(1, len(masks))]
            )
            for i in range(group)
        ]
    return terms[0]


def plane_terms(terms):
    (high, low), _ = wide_levels()
    own, by_low, by_high, corner = terms
    return total(own, across(by_low, low), across(by_high, high), across(corner, high | low))


def query_kernel(slabs, heads, w_uk, *refs):
    keys_t, grads, (grad_nope, grad_pe) = refs[:slabs], refs[slabs : 2 * slabs], refs[2 * slabs :]
    tok = grad_nope.shape[0]
    summed = dot(keys_t[0][...], grads[0][...])
    for slab in range(1, slabs):
        summed = summed + dot(keys_t[slab][...], grads[slab][...])
    for head in range(heads):
        here = slice(head * tok, (head + 1) * tok)
        grad_latent = summed[:LATENT, here].astype(BF16)
        nope = dot(w_uk[head * NOPE : (head + 1) * NOPE, :], grad_latent)
        grad_nope[:, head * NOPE : (head + 1) * NOPE] = nope.T.astype(BF16)
        grad_pe[:, head * ROPE : (head + 1) * ROPE] = summed[LATENT : LATENT + ROPE, here].T.astype(BF16)


def on_device(
    hidden,
    cotangent,
    routes,
    gates,
    offsets,
    w_gate,
    w_up,
    w_down,
    w_out,
    latent,
    rope_key,
    q_nope,
    q_pe,
    w_uk,
    w_uv,
):
    rows, width = hidden.shape
    tok = q_nope.shape[0]
    heads = q_nope.shape[1] // NOPE
    scale = 1.0 / math.sqrt(NOPE + ROPE)
    wide_size, ring = lax.axis_size("wide"), lax.axis_size("narrow")
    wide_index, ring_index = lax.axis_index("wide"), lax.axis_index("narrow")
    experts = wide_size * ring // 2
    (high, low), rest = wide_levels()
    key_width = LATENT + -(-max(ROPE, 2 * experts) // LANES) * LANES
    shape = jax.ShapeDtypeStruct
    turn = ring_index.astype(jnp.int32).reshape(1)
    (payload,) = call(
        functools.partial(pack_kernel, experts),
        [shape((2, rows, width + key_width - LATENT // 2), BF16)],
        [(turn, SMEM)] + [(value, HBM) for value in (hidden, cotangent, routes.T, gates.T, latent, rope_key.T)],
        0,
        PACK_LIMIT,
        [
            pltpu.VMEM((ROPE, tok), BF16),
            pltpu.VMEM((routes.shape[1], rows), jnp.int32),
            pltpu.VMEM((routes.shape[1], rows), F32),
            pltpu.VMEM((rows, LATENT), BF16),
            pltpu.VMEM((rows, width), BF16),
            pltpu.VMEM((rows, width), BF16),
            pltpu.VMEM((tok, ROPE), BF16),
            pltpu.SemaphoreType.DMA((6,)),
        ],
    )
    payload = payload.reshape(2 * rows, -1)
    routed, keys = routed_sum(payload, rows, w_gate[0].T, w_up[0].T, w_down[0])
    resid_grad = (cotangent.astype(F32) + routed).astype(BF16)

    order = [0, low, high, high | low]
    for level in rest:
        extra = [0, level[0]] if len(level) == 1 else [0, level[1], level[0], level[0] | level[1]]
        order = [mask ^ more for more in extra for mask in order]
    places = wide_index ^ jnp.array(order, jnp.int32)
    turns = (ring_index - jnp.arange(ring, dtype=jnp.int32)) % ring
    bases = (offsets[places][None, :] * tok + turns[:, None] * rows).reshape(len(keys), 4)
    query_base = (offsets[wide_index] * tok).reshape(1)

    columns, key_count, groups = heads * tok, keys[0].shape[0], len(keys)
    work = 2 * key_count * columns * key_width
    row = shape((1, columns), F32)
    queries, top, *made = call(
        functools.partial(score_kernel, heads, scale),
        [shape((columns, key_width), BF16), row]
        + [shape((key_count, columns), F32)] * groups
        + [shape((key_width, key_count), BF16)] * groups,
        [(bases, SMEM), (query_base, SMEM), q_nope, q_pe, w_uk, *keys],
        work * groups,
        32,
        [pltpu.VMEM((key_width, columns), BF16)],
    )
    scores, keys_t = made[:groups], made[groups:]
    pieces = [resid_grad, along(resid_grad)]
    outs_t, *probs = call(
        functools.partial(prob_kernel, groups),
        [shape((LATENT, columns), F32)] + [shape((key_count, columns), BF16)] * groups,
        [top, *scores, *keys_t],
        work * groups,
        32,
        [pltpu.VMEM((groups, key_count, columns), F32)],
    )
    for step in range(2, ring):
        tied = queries if step == 2 else outs_t
        pieces.append(along(after(pieces[-1], tied)))
    latents, latents_t, delta = call(
        functools.partial(out_kernel, heads),
        [shape((columns, LATENT), BF16), shape((LATENT, columns), BF16), row],
        [(turn, SMEM), w_out, w_uv, outs_t, *pieces],
        work,
        20,
        [pltpu.VMEM((tok, heads * VDIM), BF16)],
    )
    count = groups // ring
    grads = [None] * groups
    arrived = []
    for slabs in (range(1, ring - 1), (ring - 1, 0)):
        chosen = [slab * count + block for slab in slabs for block in range(count)]
        made = call(
            functools.partial(key_kernel, len(chosen), scale),
            [shape((key_count, columns), BF16)] * len(chosen)
            + [shape((4, len(slabs), rows, key_width), BF16)] * count,
            [queries, latents, latents_t, delta, *[keys[i] for i in chosen], *[probs[i] for i in chosen]],
            3 * work * len(chosen),
            24,
        )
        for place, group in enumerate(chosen):
            grads[group] = made[place]
        sums = owner_terms(made[len(chosen) :])
        if 0 in slabs:
            sums = [plane_terms(sums[:, place])[None] for place in range(len(slabs))]
        else:
            sums = [plane_terms(sums)]
        for place, slab in enumerate(slabs):
            moves = [(i, (i - slab) % ring) for i in range(ring)]
            part = sums[place][0] if len(sums) > 1 else sums[0][place]
            arrived.append(lax.ppermute(part, "narrow", moves) if slab else part)
    grad_q_nope, grad_q_pe = call(
        functools.partial(query_kernel, groups, heads),
        [shape(q_nope.shape, BF16), shape(q_pe.shape, BF16)],
        [w_uk, *keys_t, *grads],
        work * groups,
        24,
    )
    return (
        resid_grad,
        grad_q_nope,
        grad_q_pe,
        sum(part[:, :LATENT].astype(F32) for part in arrived),
        sum(part[:, LATENT : LATENT + ROPE].astype(F32) for part in arrived),
    )


def solution(mesh):
    return jax.shard_map(
        on_device,
        mesh=mesh,
        in_specs=(
            P(("wide", "narrow"), None),
            P(("wide", "narrow"), None),
            P(("wide", "narrow"), None),
            P(("wide", "narrow"), None),
            P(),
            P(("wide", "narrow"), None, None),
            P(("wide", "narrow"), None, None),
            P(("wide", "narrow"), None, None),
            P("narrow", None),
            P("wide", None),
            P("wide", None),
            P("wide", "narrow"),
            P("wide", "narrow"),
            P("narrow", None),
            P("narrow", None),
        ),
        out_specs=(
            P(("wide", "narrow"), None),
            P("wide", "narrow"),
            P("wide", "narrow"),
            P(("wide", "narrow"), None),
            P(("wide", "narrow"), None),
        ),
        check_vma=False,
    )
```

```python
import functools
import math

import jax
import jax.numpy as jnp
from jax import lax
from jax.experimental import pallas as pl
from jax.experimental.pallas import tpu as pltpu
from jax.sharding import PartitionSpec as P

LATENT = 512
NOPE = 128
ROPE = 64
VDIM = 128

F32 = jnp.float32
BF16 = jnp.bfloat16
CONTRACT_LAST = (((1,), (1,)), ((), ()))


def across(value, mask):
    pairs = [(source, source ^ mask) for source in range(lax.axis_size("wide"))]
    return lax.ppermute(value, "wide", pairs)


def along(value):
    size = lax.axis_size("narrow")
    return lax.ppermute(value, "narrow", [(i, (i + 1) % size) for i in range(size)])


def wide_levels():
    size = lax.axis_size("wide")
    masks = []
    mask = size // 2
    while mask:
        masks.append(mask)
        mask //= 2
    first, rest = masks[:2], masks[2:]
    return first, [rest[i : i + 2] for i in range(0, len(rest), 2)]


def gather_level(block, level):
    if len(level) == 1:
        return [block, across(block, level[0])]
    high, low = level
    by_low, by_high = across(block, low), across(block, high)
    half = block.shape[0] // 2
    corner = jnp.concatenate([across(by_low[:half], high), across(by_high[half:], low)], axis=0)
    return [block, by_low, by_high, corner]


def total(*terms):
    summed = terms[0].astype(F32)
    for term in terms[1:]:
        summed = summed + term.astype(F32)
    return summed.astype(BF16)


def scatter_level(blocks, level):
    if len(level) == 1:
        return total(blocks[0], across(blocks[1], level[0]))
    high, low = level
    own, by_low, by_high, corner = blocks
    half = own.shape[1] // 2
    from_high = across(corner[:, :half], high)
    from_low = across(corner[:, half:], low)
    by_low = jnp.concatenate([total(by_low[:, :half], from_high), by_low[:, half:]], axis=1)
    by_high = jnp.concatenate([by_high[:, :half], total(by_high[:, half:], from_low)], axis=1)
    return total(own, across(by_low, low), across(by_high, high))

LANES = 128
PACK_LIMIT = 56
VMEM = pl.BlockSpec(memory_space=pltpu.VMEM)
SMEM = pl.BlockSpec(memory_space=pltpu.SMEM)
HBM = pl.BlockSpec(memory_space=pltpu.HBM)


def dot(left, right):
    return jnp.dot(left, right, preferred_element_type=F32)


def dot_last(left, right):
    return lax.dot_general(left, right, CONTRACT_LAST, preferred_element_type=F32)


def call(kernel, outs, ins, flops, limit, scratch=()):
    specs = [entry[1] if isinstance(entry, tuple) else VMEM for entry in ins]
    arrays = [entry[0] if isinstance(entry, tuple) else entry for entry in ins]
    moved = sum(math.prod(out.shape) * out.dtype.itemsize for out in outs)
    moved += sum(array.size * array.dtype.itemsize for array in arrays)
    return pl.pallas_call(
        kernel,
        out_shape=outs,
        in_specs=specs,
        out_specs=[VMEM] * len(outs),
        scratch_shapes=list(scratch),
        compiler_params=pltpu.CompilerParams(vmem_limit_bytes=limit * 2**20),
        cost_estimate=pl.CostEstimate(flops=flops, bytes_accessed=moved, transcendentals=0),
    )(*arrays)


def pack_kernel(experts, index, hidden, cotangent, routes, gates, latent, rope, out, *scratch):
    *held, turned, sems = scratch
    rows, width = hidden.shape
    half = latent.shape[1] // 2
    tail = out.shape[2] - width - half
    place = pl.ds(pl.multiple_of(index[0] * rows, rows), rows)
    sources = [rope, routes, gates, latent.at[place, :], hidden, cotangent]
    copies = [
        pltpu.make_async_copy(source, target, sems.at[i])
        for i, (source, target) in enumerate(zip(sources, held))
    ]
    for copy in copies:
        copy.start()
    for copy in copies[:3]:
        copy.wait()
    rope_held, routes_held, gates_held, latent_held, hidden_held, cotangent_held = held
    turned[...] = rope_held[...].T
    out[0, :, width + half :] = jnp.zeros((rows, tail), BF16)
    out[0, :, width + half : width + half + ROPE] = turned[place, :]
    line = lax.broadcasted_iota(jnp.int32, (tail, rows), 0)
    first = jnp.zeros((tail, rows), F32)
    second = jnp.zeros((tail, rows), F32)
    for k in range(routes.shape[0]):
        chosen, weight = routes_held[k : k + 1, :], gates_held[k : k + 1, :]
        first = first + jnp.where(line == chosen, weight, 0.0)
        second = second + jnp.where(line == chosen + experts, weight, 0.0)
    second = second - second.astype(BF16).astype(F32)
    out[1, :, width + half :] = (first + second).T.astype(BF16)
    for copy in copies[3:]:
        copy.wait()
    out[0, :, width : width + half] = latent_held[:, :half]
    out[1, :, width : width + half] = latent_held[:, half:]
    out[0, :, :width] = hidden_held[...]
    out[1, :, :width] = cotangent_held[...]


def expert_kernel(experts, expert_ref, tokens, w_gate, w_up, w_down, keys, out):
    pieces, _, rows, wide = tokens.shape
    width = w_down.shape[1]
    merged = pieces * rows
    tail = keys.shape[1] - LATENT
    half = wide - tail
    x_rows = tokens[:, 0, :, :width].reshape(merged, width)
    dy_rows = tokens[:, 1, :, :width].reshape(merged, width)
    keys[:, : half - width] = tokens[:, 0, :, width:half].reshape(merged, half - width)
    keys[:, half - width : LATENT] = tokens[:, 1, :, width:half].reshape(merged, half - width)
    keys[:, LATENT:] = tokens[:, 0, :, half:].reshape(merged, tail)
    parts = tokens[:, 1, :, half:].reshape(merged, tail).astype(F32)
    lane = lax.broadcasted_iota(jnp.int32, (merged, tail), 1)
    mine = (lane == expert_ref[0]) | (lane == expert_ref[0] + experts)
    gate = jnp.sum(jnp.where(mine, parts, 0.0), axis=1, keepdims=True)
    pre_gate = dot_last(x_rows, w_gate[...])
    up_value = dot_last(x_rows, w_up[...])
    grad_hidden = gate * dot_last(dy_rows, w_down[...])
    sigmoid_gate = jax.nn.sigmoid(pre_gate)
    scaled = grad_hidden * sigmoid_gate
    grad_gate = scaled * up_value * (1.0 + pre_gate * (1.0 - sigmoid_gate))
    grad_up = scaled * pre_gate
    partial_grad = dot(grad_gate.astype(BF16), w_gate[...]) + dot(grad_up.astype(BF16), w_up[...])
    out[...] = partial_grad.astype(BF16)


def after(value, *earlier):
    return lax.optimization_barrier((value, *earlier))[0]


def routed_sum(payload, rows, w_gate, w_up, w_down):
    wide_size, ring = lax.axis_size("wide"), lax.axis_size("narrow")
    wide_index, ring_index = lax.axis_index("wide"), lax.axis_index("narrow")
    experts = wide_size * ring // 2
    expert = ((wide_index * ring + ring_index) // 2).astype(jnp.int32).reshape(1)
    wide, width = payload.shape[1], w_down.shape[1]
    (high, low), rest = wide_levels()
    key_width = LATENT + wide - width - LATENT // 2

    def experts_of(block):
        return call(
            functools.partial(expert_kernel, experts),
            [jax.ShapeDtypeStruct((4 * rows, key_width), BF16), jax.ShapeDtypeStruct((4 * rows, width), BF16)],
            [(expert, SMEM), block.reshape(4, 2, rows, wide), w_gate, w_up, w_down],
            40 * rows * w_down.size,
            14,
        )

    def spread(block):
        blocks = [block]
        for level in rest:
            blocks = [piece for one in zip(*[gather_level(b, level) for b in blocks]) for piece in one]
        return blocks

    def collect(sums):
        for level in reversed(rest):
            group = len(sums) // 2 ** len(level)
            sums = [
                scatter_level([sums[i + group * j] for j in range(2 ** len(level))], level)
                for i in range(group)
            ]
        return sums[0]

    def together(*values):
        return list(lax.optimization_barrier(values))

    def with_room(column):
        return jnp.concatenate([column, column[:rows]], axis=0)

    def filled(room, half):
        return lax.dynamic_update_slice_in_dim(room, half, 2 * rows, 0)

    slabs, results, sums = [], [], []
    column, rooms, sides, former = payload, None, None, None
    for turn in range(ring + 1):
        if turn == 0:
            moving = [across(column, low), across(column, high), along(column)]
            beside = []
        else:
            halves = [sides[1][rows:], sides[0][:rows]]
            sent = [filled(*pair) for pair in zip(rooms, halves)] if turn < ring else halves
            moving = [across(sent[0], low), across(sent[1], high)]
            if turn < ring - 1:
                moving.append(along(column))
            beside = []
        if turn > 1:
            blocks = spread(after(slabs[turn - 2], *sent))
            results.append([experts_of(block) for block in blocks])
            beside += [result[1] for result in results[-1]][: None if turn < ring else 1]
        if turn > 2:
            sums.append(collect([result[1] for result in results[turn - 3]]))
            beside.append(sums[-1])
        if turn < ring - 1:
            beside += [with_room(moving[2]), with_room(moving[2])]
        done = together(*moving, *beside)
        if turn > 0:
            corner = [part[-rows:] for part in done[:2]]
            slabs.append(jnp.concatenate([former, *sides, corner[1], corner[0]], axis=0))
        if turn < ring:
            sides = [part[: 2 * rows] for part in done[:2]]
        former = column
        if turn < ring - 1:
            column, rooms = done[2], done[-2:]

    def parts_of(step):
        return list(sums[step].reshape(4, rows, width))

    last = ring - 1
    link = corner = None
    for step in range(1, last - 1):
        own, by_low, by_high, far = parts_of(step)
        moving = [
            across(by_low, low),
            across(by_high, high),
            along(far if corner is None else total(far, corner)),
        ]
        if link is not None:
            moving.append(along(link))
        count, beside = len(moving), []
        if step == last - 2:
            first, *others = spread(slabs[last])
            before = [result[1] for result in results[last - 1]]
            beside = [*before[1:], *others]
        done = together(*moving, *beside)
        corner = done[2]
        link = total(own, *done[:2], *done[3:count])
    others = [experts_of(block) for block in done[-len(others) :]]
    sums.append(collect(before))
    home, home_low, home_high, home_far = parts_of(0)
    link, home_far, sums[last - 1], *_ = together(
        along(link), across(home_far, high | low), sums[last - 1], *[result[1] for result in others]
    )
    own, by_low, by_high, far = parts_of(last - 1)
    first = experts_of(after(first, home_far))
    results.append([first, *others])
    sums.append(collect([result[1] for result in results[last]]))
    by_low, by_high, corner, sums[last] = together(
        across(by_low, low), across(by_high, high), along(total(far, corner)), sums[last]
    )
    link = total(own, by_low, by_high, link)
    own, by_low, by_high, far = parts_of(last)
    done = together(
        across(by_low, low),
        across(by_high, high),
        across(total(far, corner), high | low),
        along(link),
    )
    link = total(own, *done)
    done = together(along(link), across(home_low, low), across(home_high, high))
    summed = sum(part.astype(F32) for part in (home, home_far, *done))
    return summed, [result[0] for slab in results for result in slab]


def before_kernel(heads, scale, index, bases, query_base, q_nope, q_pe, w_uk, *refs):
    groups, pieces = bases.shape
    keys, (queries, outs_t, *rest), (nope, pe, queries_t, scores) = refs[:groups], refs[groups:-4], refs[-4:]
    probs, keys_t = rest[:groups], rest[groups:]
    tok = q_nope.shape[0]
    key_count, key_width = keys[0].shape
    columns = heads * tok
    rows = key_count // pieces
    ring = tok // rows
    for step in range(ring):
        place = lax.rem(index[0] + (ring - step), jnp.int32(ring))
        source, target = pl.ds(pl.multiple_of(place * rows, rows), rows), pl.ds(step * rows, rows)
        nope[target, :] = q_nope[source, :]
        pe[target, :] = q_pe[source, :]
    queries[:, LATENT:] = jnp.zeros((columns, key_width - LATENT), BF16)
    for head in range(heads):
        made = dot(
            nope[:, head * NOPE : (head + 1) * NOPE], w_uk[head * NOPE : (head + 1) * NOPE, :]
        ).astype(BF16)
        for step in range(ring):
            here = pl.ds((step * heads + head) * rows, rows)
            part = slice(step * rows, (step + 1) * rows)
            queries[here, :LATENT] = made[part]
            queries[here, LATENT : LATENT + ROPE] = pe[part, head * ROPE : (head + 1) * ROPE]
    queries_t[...] = queries[...].T
    column = lax.broadcasted_iota(jnp.int32, (1, columns), 1)
    place = lax.rem(index[0] + (ring - lax.div(column, jnp.int32(heads * rows))), jnp.int32(ring))
    position = query_base[0] + place * rows + lax.rem(column, jnp.int32(rows))
    ahead = lax.broadcasted_iota(jnp.int32, (rows, columns), 0) - position
    highest = jnp.full((1, columns), -1e30, F32)
    for group in range(groups):
        raw = dot(keys[group][...], queries_t[...])
        for piece in range(pieces):
            here = slice(piece * rows, (piece + 1) * rows)
            shown = ahead + bases[group, piece] <= 0
            masked = jnp.where(shown, raw[here, :] * scale, -1e30)
            scores[group, here, :] = masked
            highest = jnp.maximum(highest, jnp.max(masked, axis=0, keepdims=True))
        keys_t[group][...] = keys[group][...].T
    norm = jnp.zeros((1, columns), F32)
    for group in range(groups):
        grown = jnp.exp(scores[group] - highest)
        scores[group] = grown
        norm = norm + jnp.sum(grown, axis=0, keepdims=True)
    inverse = 1.0 / norm
    for group in range(groups):
        probs[group][...] = (scores[group] * inverse).astype(BF16)
        part = dot(keys_t[group][:LATENT, :], probs[group][...])
        if group == 0:
            outs_t[...] = part
        else:
            outs_t[...] += part


def out_kernel(heads, start, w_out, w_uv, outs_t, *refs):
    resid, (latents, latents_t, delta) = refs[:-3], refs[-3:]
    rows = resid[0].shape[0]
    moved = jnp.concatenate([part[...] for part in resid], axis=0)
    grad_out = dot_last(moved, w_out[...]).astype(BF16)
    for head in range(heads):
        made = dot(
            grad_out[:, head * VDIM : (head + 1) * VDIM], w_uv[head * VDIM : (head + 1) * VDIM, :]
        ).astype(BF16)
        for step in range(len(resid)):
            latents[pl.ds((step * heads + head) * rows, rows), :] = made[step * rows : (step + 1) * rows]
    turned = latents[...].T
    latents_t[...] = turned
    first = start * heads * rows
    means = outs_t[:, first : first + turned.shape[1]]
    delta[...] = jnp.sum(means * turned.astype(F32), axis=0, keepdims=True)


def key_kernel(groups, start, added, scale, queries, latents, latents_t, delta, *refs):
    keys, probs, refs = refs[:groups], refs[groups : 2 * groups], refs[2 * groups :]
    before, refs = (refs[:groups], refs[groups:]) if added else (None, refs)
    grads, terms = refs[:groups], refs[groups:]
    key_count, key_width = keys[0].shape
    here = slice(start, start + latents.shape[0])
    for group in range(groups):
        chances = probs[group][:, here]
        grad_probs = dot(keys[group][:, :LATENT], latents_t[...])
        grads[group][...] = (scale * chances.astype(F32) * (grad_probs - delta[...])).astype(BF16)
        term = dot(grads[group][...], queries[here, :])
        term_latent = term[:, :LATENT] + dot(chances, latents[...])
        if not added:
            terms[group][:, :LATENT] = term_latent
            terms[group][:, LATENT:] = term[:, LATENT:]
            continue
        out, place = terms[group % len(terms)], group // len(terms)
        pieces, _, rows, _ = out.shape
        out[:, place, :, :LATENT] = (
            (term_latent + before[group][:, :LATENT]).astype(BF16).reshape(pieces, rows, LATENT)
        )
        out[:, place, :, LATENT:] = (
            (term[:, LATENT:] + before[group][:, LATENT:])
            .astype(BF16)
            .reshape(pieces, rows, key_width - LATENT)
        )


def owner_terms(terms):
    (high, low), rest = wide_levels()
    for level in reversed(rest):
        masks = [0, level[0]] if len(level) == 1 else [0, level[1], level[0], level[0] | level[1]]
        group = len(terms) // len(masks)
        terms = [
            total(
                terms[i], *[across(terms[i + group * j], masks[j]) for j in range(1, len(masks))]
            )
            for i in range(group)
        ]
    return terms[0]


def plane_terms(terms):
    (high, low), _ = wide_levels()
    own, by_low, by_high, corner = terms
    return total(own, across(by_low, low), across(by_high, high), across(corner, high | low))


def query_kernel(groups, heads, index, w_uk, *refs):
    keys_t, refs = refs[:groups], refs[groups:]
    early, late, (grad_nope, grad_pe) = refs[:groups], refs[groups : 2 * groups], refs[2 * groups :]
    tok = grad_nope.shape[0]
    rows = late[0].shape[1] // heads
    ring = tok // rows
    summed = []
    for grads in (early, late):
        part = dot(keys_t[0][...], grads[0][...])
        for group in range(1, groups):
            part = part + dot(keys_t[group][...], grads[group][...])
        summed.append(part.T.astype(BF16))
    summed = jnp.concatenate(summed, axis=0)
    for head in range(heads):
        taken = [summed[(step * heads + head) * rows : (step * heads + head + 1) * rows] for step in range(ring)]
        nope = dot_last(
            jnp.concatenate(taken, axis=0)[:, :LATENT], w_uk[head * NOPE : (head + 1) * NOPE, :]
        ).astype(BF16)
        for step in range(ring):
            place = lax.rem(index[0] + (ring - step), jnp.int32(ring))
            here = pl.ds(pl.multiple_of(place * rows, rows), rows)
            grad_nope[here, head * NOPE : (head + 1) * NOPE] = nope[step * rows : (step + 1) * rows]
            grad_pe[here, head * ROPE : (head + 1) * ROPE] = taken[step][:, LATENT : LATENT + ROPE]


def on_device(
    hidden,
    cotangent,
    routes,
    gates,
    offsets,
    w_gate,
    w_up,
    w_down,
    w_out,
    latent,
    rope_key,
    q_nope,
    q_pe,
    w_uk,
    w_uv,
):
    rows, width = hidden.shape
    tok = q_nope.shape[0]
    heads = q_nope.shape[1] // NOPE
    scale = 1.0 / math.sqrt(NOPE + ROPE)
    wide_size, ring = lax.axis_size("wide"), lax.axis_size("narrow")
    wide_index, ring_index = lax.axis_index("wide"), lax.axis_index("narrow")
    experts = wide_size * ring // 2
    (high, low), rest = wide_levels()
    key_width = LATENT + -(-max(ROPE, 2 * experts) // LANES) * LANES
    shape = jax.ShapeDtypeStruct
    turn = ring_index.astype(jnp.int32).reshape(1)
    (payload,) = call(
        functools.partial(pack_kernel, experts),
        [shape((2, rows, width + key_width - LATENT // 2), BF16)],
        [(turn, SMEM)] + [(value, HBM) for value in (hidden, cotangent, routes.T, gates.T, latent, rope_key.T)],
        0,
        PACK_LIMIT,
        [
            pltpu.VMEM((ROPE, tok), BF16),
            pltpu.VMEM((routes.shape[1], rows), jnp.int32),
            pltpu.VMEM((routes.shape[1], rows), F32),
            pltpu.VMEM((rows, LATENT), BF16),
            pltpu.VMEM((rows, width), BF16),
            pltpu.VMEM((rows, width), BF16),
            pltpu.VMEM((tok, ROPE), BF16),
            pltpu.SemaphoreType.DMA((6,)),
        ],
    )
    payload = payload.reshape(2 * rows, -1)
    order = [0, low, high, high | low]
    for level in rest:
        extra = [0, level[0]] if len(level) == 1 else [0, level[1], level[0], level[0] | level[1]]
        order = [mask ^ more for more in extra for mask in order]
    places = wide_index ^ jnp.array(order, jnp.int32)
    turns = (ring_index - jnp.arange(ring, dtype=jnp.int32)) % ring
    bases = (offsets[places][None, :] * tok + turns[:, None] * rows).reshape(-1, 4)
    query_base = (offsets[wide_index] * tok).reshape(1)
    groups = bases.shape[0]
    columns, key_count = heads * tok, 4 * rows
    work = 2 * key_count * columns * key_width
    row = shape((1, columns), F32)
    routed, keys = routed_sum(payload, rows, w_gate[0].T, w_up[0].T, w_down[0])
    resid_grad = (cotangent.astype(F32) + routed).astype(BF16)
    queries, outs_t, *made = call(
        functools.partial(before_kernel, heads, scale),
        [shape((columns, key_width), BF16), shape((LATENT, columns), F32)]
        + [shape((key_count, columns), BF16)] * groups
        + [shape((key_width, key_count), BF16)] * groups,
        [(turn, SMEM), (bases, SMEM), (query_base, SMEM), q_nope, q_pe, w_uk, *keys],
        2 * work * groups,
        24,
        [
            pltpu.VMEM(q_nope.shape, BF16),
            pltpu.VMEM(q_pe.shape, BF16),
            pltpu.VMEM((key_width, columns), BF16),
            pltpu.VMEM((groups, key_count, columns), F32),
        ],
    )
    probs, keys_t = made[:groups], made[groups:]

    pieces = [resid_grad, along(resid_grad)]
    for step in range(2, ring):
        pieces.append(along(after(pieces[-1], queries) if step == 2 else pieces[-1]))

    def latents_of(start, stop):
        size = (stop - start) * heads * rows
        return call(
            functools.partial(out_kernel, heads, start),
            [shape((size, LATENT), BF16), shape((LATENT, size), BF16), shape((1, size), F32)],
            [w_out, w_uv, outs_t, *pieces[start:stop]],
            work,
            12,
        )

    part = heads * rows
    early = latents_of(0, ring - 1)
    made = call(
        functools.partial(key_kernel, groups, 0, False, scale),
        [shape((key_count, columns - part), BF16)] * groups + [shape((key_count, key_width), F32)] * groups,
        [queries, *early, *keys, *probs],
        3 * work * groups,
        20,
    )
    grads, before = made[:groups], made[groups:]
    late = latents_of(ring - 1, ring)
    count = groups // ring
    late_grads = [None] * groups
    arrived = []
    for slabs in (range(1, ring - 1), (ring - 1, 0)):
        chosen = [slab * count + block for slab in slabs for block in range(count)]
        made = call(
            functools.partial(key_kernel, len(chosen), columns - part, True, scale),
            [shape((key_count, part), BF16)] * len(chosen)
            + [shape((4, len(slabs), rows, key_width), BF16)] * count,
            [queries, *late]
            + [values[i] for values in (keys, probs, before) for i in chosen],
            work * len(chosen),
            16,
        )
        for place, group in enumerate(chosen):
            late_grads[group] = made[place]
        sums = owner_terms(made[len(chosen) :])
        if 0 in slabs:
            sums = [plane_terms(sums[:, place])[None] for place in range(len(slabs))]
        else:
            sums = [plane_terms(sums)]
        for place, slab in enumerate(slabs):
            moves = [(i, (i - slab) % ring) for i in range(ring)]
            moved = sums[place][0] if len(sums) > 1 else sums[0][place]
            arrived.append(lax.ppermute(moved, "narrow", moves) if slab else moved)
    grad_q_nope, grad_q_pe = call(
        functools.partial(query_kernel, groups, heads),
        [shape(q_nope.shape, BF16), shape(q_pe.shape, BF16)],
        [(turn, SMEM), w_uk, *keys_t, *grads, *late_grads],
        work * groups,
        16,
    )
    return (
        resid_grad,
        grad_q_nope,
        grad_q_pe,
        sum(part[:, :LATENT].astype(F32) for part in arrived),
        sum(part[:, LATENT : LATENT + ROPE].astype(F32) for part in arrived),
    )


def solution(mesh):
    return jax.shard_map(
        on_device,
        mesh=mesh,
        in_specs=(
            P(("wide", "narrow"), None),
            P(("wide", "narrow"), None),
            P(("wide", "narrow"), None),
            P(("wide", "narrow"), None),
            P(),
            P(("wide", "narrow"), None, None),
            P(("wide", "narrow"), None, None),
            P(("wide", "narrow"), None, None),
            P("narrow", None),
            P("wide", None),
            P("wide", None),
            P("wide", "narrow"),
            P("wide", "narrow"),
            P("narrow", None),
            P("narrow", None),
        ),
        out_specs=(
            P(("wide", "narrow"), None),
            P("wide", "narrow"),
            P("wide", "narrow"),
            P(("wide", "narrow"), None),
            P(("wide", "narrow"), None),
        ),
        check_vma=False,
    )
```

```python
import functools
import math

import jax
import jax.numpy as jnp
from jax import lax
from jax.experimental import pallas as pl
from jax.experimental.pallas import tpu as pltpu
from jax.sharding import PartitionSpec as P

LATENT = 512
NOPE = 128
ROPE = 64
VDIM = 128

F32 = jnp.float32
BF16 = jnp.bfloat16
CONTRACT_LAST = (((1,), (1,)), ((), ()))


def across(value, mask):
    pairs = [(source, source ^ mask) for source in range(lax.axis_size("wide"))]
    return lax.ppermute(value, "wide", pairs)


def along(value):
    size = lax.axis_size("narrow")
    return lax.ppermute(value, "narrow", [(i, (i + 1) % size) for i in range(size)])


def wide_levels():
    size = lax.axis_size("wide")
    masks = []
    mask = size // 2
    while mask:
        masks.append(mask)
        mask //= 2
    first, rest = masks[:2], masks[2:]
    return first, [rest[i : i + 2] for i in range(0, len(rest), 2)]


def gather_level(block, level):
    if len(level) == 1:
        return [block, across(block, level[0])]
    high, low = level
    by_low, by_high = across(block, low), across(block, high)
    half = block.shape[0] // 2
    corner = jnp.concatenate([across(by_low[:half], high), across(by_high[half:], low)], axis=0)
    return [block, by_low, by_high, corner]


def total(*terms):
    summed = terms[0].astype(F32)
    for term in terms[1:]:
        summed = summed + term.astype(F32)
    return summed.astype(BF16)


def scatter_level(blocks, level):
    if len(level) == 1:
        return total(blocks[0], across(blocks[1], level[0]))
    high, low = level
    own, by_low, by_high, corner = blocks
    half = own.shape[1] // 2
    from_high = across(corner[:, :half], high)
    from_low = across(corner[:, half:], low)
    by_low = jnp.concatenate([total(by_low[:, :half], from_high), by_low[:, half:]], axis=1)
    by_high = jnp.concatenate([by_high[:, :half], total(by_high[:, half:], from_low)], axis=1)
    return total(own, across(by_low, low), across(by_high, high))

LANES = 128
PACK_LIMIT = 56
VMEM = pl.BlockSpec(memory_space=pltpu.VMEM)
SMEM = pl.BlockSpec(memory_space=pltpu.SMEM)
HBM = pl.BlockSpec(memory_space=pltpu.HBM)


def dot(left, right):
    return jnp.dot(left, right, preferred_element_type=F32)


def dot_last(left, right):
    return lax.dot_general(left, right, CONTRACT_LAST, preferred_element_type=F32)


def call(kernel, outs, ins, flops, limit, scratch=()):
    specs = [entry[1] if isinstance(entry, tuple) else VMEM for entry in ins]
    arrays = [entry[0] if isinstance(entry, tuple) else entry for entry in ins]
    moved = sum(math.prod(out.shape) * out.dtype.itemsize for out in outs)
    moved += sum(array.size * array.dtype.itemsize for array in arrays)
    return pl.pallas_call(
        kernel,
        out_shape=outs,
        in_specs=specs,
        out_specs=[VMEM] * len(outs),
        scratch_shapes=list(scratch),
        compiler_params=pltpu.CompilerParams(vmem_limit_bytes=limit * 2**20),
        cost_estimate=pl.CostEstimate(flops=flops, bytes_accessed=moved, transcendentals=0),
    )(*arrays)


def pack_kernel(experts, index, hidden, cotangent, routes, gates, latent, rope, out, *scratch):
    *held, turned, sems = scratch
    rows, width = hidden.shape
    half = latent.shape[1] // 2
    tail = out.shape[2] - width - half
    place = pl.ds(pl.multiple_of(index[0] * rows, rows), rows)
    sources = [rope, routes, gates, latent.at[place, :], hidden, cotangent]
    copies = [
        pltpu.make_async_copy(source, target, sems.at[i])
        for i, (source, target) in enumerate(zip(sources, held))
    ]
    for copy in copies:
        copy.start()
    for copy in copies[:3]:
        copy.wait()
    rope_held, routes_held, gates_held, latent_held, hidden_held, cotangent_held = held
    turned[...] = rope_held[...].T
    out[0, :, width + half :] = jnp.zeros((rows, tail), BF16)
    out[0, :, width + half : width + half + ROPE] = turned[place, :]
    line = lax.broadcasted_iota(jnp.int32, (tail, rows), 0)
    first = jnp.zeros((tail, rows), F32)
    second = jnp.zeros((tail, rows), F32)
    for k in range(routes.shape[0]):
        chosen, weight = routes_held[k : k + 1, :], gates_held[k : k + 1, :]
        first = first + jnp.where(line == chosen, weight, 0.0)
        second = second + jnp.where(line == chosen + experts, weight, 0.0)
    second = second - second.astype(BF16).astype(F32)
    out[1, :, width + half :] = (first + second).T.astype(BF16)
    for copy in copies[3:]:
        copy.wait()
    out[0, :, width : width + half] = latent_held[:, :half]
    out[1, :, width : width + half] = latent_held[:, half:]
    out[0, :, :width] = hidden_held[...]
    out[1, :, :width] = cotangent_held[...]


def expert_kernel(experts, expert_ref, tokens, w_gate, w_up, w_down, keys, out):
    pieces, _, rows, wide = tokens.shape
    width = w_down.shape[1]
    merged = pieces * rows
    tail = keys.shape[1] - LATENT
    half = wide - tail
    x_rows = tokens[:, 0, :, :width].reshape(merged, width)
    dy_rows = tokens[:, 1, :, :width].reshape(merged, width)
    keys[:, : half - width] = tokens[:, 0, :, width:half].reshape(merged, half - width)
    keys[:, half - width : LATENT] = tokens[:, 1, :, width:half].reshape(merged, half - width)
    keys[:, LATENT:] = tokens[:, 0, :, half:].reshape(merged, tail)
    parts = tokens[:, 1, :, half:].reshape(merged, tail).astype(F32)
    lane = lax.broadcasted_iota(jnp.int32, (merged, tail), 1)
    mine = (lane == expert_ref[0]) | (lane == expert_ref[0] + experts)
    gate = jnp.sum(jnp.where(mine, parts, 0.0), axis=1, keepdims=True)
    pre_gate = dot_last(x_rows, w_gate[...])
    up_value = dot_last(x_rows, w_up[...])
    grad_hidden = gate * dot_last(dy_rows, w_down[...])
    sigmoid_gate = jax.nn.sigmoid(pre_gate)
    scaled = grad_hidden * sigmoid_gate
    grad_gate = scaled * up_value * (1.0 + pre_gate * (1.0 - sigmoid_gate))
    grad_up = scaled * pre_gate
    partial_grad = dot(grad_gate.astype(BF16), w_gate[...]) + dot(grad_up.astype(BF16), w_up[...])
    out[...] = partial_grad.astype(BF16)


def after(value, *earlier):
    return lax.optimization_barrier((value, *earlier))[0]


def routed_sum(payload, rows, w_gate, w_up, w_down):
    wide_size, ring = lax.axis_size("wide"), lax.axis_size("narrow")
    wide_index, ring_index = lax.axis_index("wide"), lax.axis_index("narrow")
    experts = wide_size * ring // 2
    expert = ((wide_index * ring + ring_index) // 2).astype(jnp.int32).reshape(1)
    wide, width = payload.shape[1], w_down.shape[1]
    (high, low), rest = wide_levels()
    key_width = LATENT + wide - width - LATENT // 2

    def experts_of(block):
        return call(
            functools.partial(expert_kernel, experts),
            [jax.ShapeDtypeStruct((4 * rows, key_width), BF16), jax.ShapeDtypeStruct((4 * rows, width), BF16)],
            [(expert, SMEM), block.reshape(4, 2, rows, wide), w_gate, w_up, w_down],
            40 * rows * w_down.size,
            14,
        )

    def spread(block):
        blocks = [block]
        for level in rest:
            blocks = [piece for one in zip(*[gather_level(b, level) for b in blocks]) for piece in one]
        return blocks

    def collect(sums):
        if len(sums) == 2:
            moved = across(sums[1], rest[0][0])
            return [
                total(sums[0][i * rows : (i + 1) * rows], moved[i * rows : (i + 1) * rows]) for i in range(4)
            ]
        for level in reversed(rest):
            group = len(sums) // 2 ** len(level)
            sums = [
                scatter_level([sums[i + group * j] for j in range(2 ** len(level))], level)
                for i in range(group)
            ]
        return list(sums[0].reshape(4, rows, width))

    def together(*values):
        return list(lax.optimization_barrier(values))

    def with_room(column):
        return jnp.concatenate([column, column[:rows]], axis=0)

    def filled(room, half):
        return lax.dynamic_update_slice_in_dim(room, half, 2 * rows, 0)

    slabs, results, sums = [], [], []
    column, rooms, sides, former = payload, None, None, None
    for turn in range(ring + 1):
        if turn == 0:
            moving = [across(column, low), across(column, high), along(column)]
            beside = []
        else:
            halves = [sides[1][rows:], sides[0][:rows]]
            sent = [filled(*pair) for pair in zip(rooms, halves)] if turn < ring else halves
            moving = [across(sent[0], low), across(sent[1], high)]
            if turn < ring - 1:
                moving.append(along(column))
            beside = []
        if turn > 1:
            blocks = spread(after(slabs[turn - 2], *sent))
            results.append([experts_of(block) for block in blocks])
            beside += [result[1] for result in results[-1]][: None if turn < ring else 1]
        if turn > 2:
            sums.append(collect([result[1] for result in results[turn - 3]]))
            beside += sums[-1]
        if turn < ring - 1:
            beside += [with_room(moving[2]), with_room(moving[2])]
        done = together(*moving, *beside)
        if turn > 0:
            corner = [part[-rows:] for part in done[:2]]
            slabs.append(jnp.concatenate([former, *sides, corner[1], corner[0]], axis=0))
        if turn < ring:
            sides = [part[: 2 * rows] for part in done[:2]]
        former = column
        if turn < ring - 1:
            column, rooms = done[2], done[-2:]

    def parts_of(step):
        return sums[step]

    last = ring - 1
    link = corner = None
    for step in range(1, last - 1):
        own, by_low, by_high, far = parts_of(step)
        moving = [
            across(by_low, low),
            across(by_high, high),
            along(far if corner is None else total(far, corner)),
        ]
        if link is not None:
            moving.append(along(link))
        count, beside = len(moving), []
        if step == last - 2:
            first, *others = spread(slabs[last])
            before = [result[1] for result in results[last - 1]]
            beside = [*before[1:], *others]
        done = together(*moving, *beside)
        corner = done[2]
        link = total(own, *done[:2], *done[3:count])
    others = [experts_of(block) for block in done[-len(others) :]]
    sums.append(collect(before))
    home, home_low, home_high, home_far = parts_of(0)
    link, home_far, *done = together(
        along(link), across(home_far, high | low), *sums[last - 1], *[result[1] for result in others]
    )
    sums[last - 1] = done[:4]
    own, by_low, by_high, far = parts_of(last - 1)
    first = experts_of(after(first, home_far))
    results.append([first, *others])
    sums.append(collect([result[1] for result in results[last]]))
    by_low, by_high, corner, *sums[last] = together(
        across(by_low, low), across(by_high, high), along(total(far, corner)), *sums[last]
    )
    link = total(own, by_low, by_high, link)
    own, by_low, by_high, far = parts_of(last)
    done = together(
        across(by_low, low),
        across(by_high, high),
        across(total(far, corner), high | low),
        along(link),
    )
    link = total(own, *done)
    done = together(along(link), across(home_low, low), across(home_high, high))
    summed = sum(part.astype(F32) for part in (home, home_far, *done))
    return summed, [result[0] for slab in results for result in slab]


def before_kernel(heads, scale, index, bases, query_base, q_nope, q_pe, w_uk, *refs):
    groups, pieces = bases.shape
    keys, (queries, outs_t, *rest), (nope, pe, queries_t, scores) = refs[:groups], refs[groups:-4], refs[-4:]
    probs, keys_t = rest[:groups], rest[groups:]
    tok = q_nope.shape[0]
    key_count, key_width = keys[0].shape
    columns = heads * tok
    rows = key_count // pieces
    ring = tok // rows
    for step in range(ring):
        place = lax.rem(index[0] + (ring - step), jnp.int32(ring))
        source, target = pl.ds(pl.multiple_of(place * rows, rows), rows), pl.ds(step * rows, rows)
        nope[target, :] = q_nope[source, :]
        pe[target, :] = q_pe[source, :]
    queries[:, LATENT:] = jnp.zeros((columns, key_width - LATENT), BF16)
    for head in range(heads):
        made = dot(
            nope[:, head * NOPE : (head + 1) * NOPE], w_uk[head * NOPE : (head + 1) * NOPE, :]
        ).astype(BF16)
        for step in range(ring):
            here = pl.ds((step * heads + head) * rows, rows)
            part = slice(step * rows, (step + 1) * rows)
            queries[here, :LATENT] = made[part]
            queries[here, LATENT : LATENT + ROPE] = pe[part, head * ROPE : (head + 1) * ROPE]
    queries_t[...] = queries[...].T
    column = lax.broadcasted_iota(jnp.int32, (1, columns), 1)
    place = lax.rem(index[0] + (ring - lax.div(column, jnp.int32(heads * rows))), jnp.int32(ring))
    position = query_base[0] + place * rows + lax.rem(column, jnp.int32(rows))
    ahead = lax.broadcasted_iota(jnp.int32, (rows, columns), 0) - position
    highest = jnp.full((1, columns), -1e30, F32)
    for group in range(groups):
        raw = dot(keys[group][...], queries_t[...])
        for piece in range(pieces):
            here = slice(piece * rows, (piece + 1) * rows)
            shown = ahead + bases[group, piece] <= 0
            masked = jnp.where(shown, raw[here, :] * scale, -1e30)
            scores[group, here, :] = masked
            highest = jnp.maximum(highest, jnp.max(masked, axis=0, keepdims=True))
        keys_t[group][...] = keys[group][...].T
    norm = jnp.zeros((1, columns), F32)
    for group in range(groups):
        grown = jnp.exp(scores[group] - highest)
        scores[group] = grown
        norm = norm + jnp.sum(grown, axis=0, keepdims=True)
    inverse = 1.0 / norm
    for group in range(groups):
        probs[group][...] = (scores[group] * inverse).astype(BF16)
        part = dot(keys_t[group][:LATENT, :], probs[group][...])
        if group == 0:
            outs_t[...] = part
        else:
            outs_t[...] += part


def out_kernel(heads, start, w_out, w_uv, outs_t, *refs):
    resid, (latents, latents_t, delta) = refs[:-3], refs[-3:]
    rows = resid[0].shape[0]
    moved = jnp.concatenate([part[...] for part in resid], axis=0)
    grad_out = dot_last(moved, w_out[...]).astype(BF16)
    for head in range(heads):
        made = dot(
            grad_out[:, head * VDIM : (head + 1) * VDIM], w_uv[head * VDIM : (head + 1) * VDIM, :]
        ).astype(BF16)
        for step in range(len(resid)):
            latents[pl.ds((step * heads + head) * rows, rows), :] = made[step * rows : (step + 1) * rows]
    turned = latents[...].T
    latents_t[...] = turned
    first = start * heads * rows
    means = outs_t[:, first : first + turned.shape[1]]
    delta[...] = jnp.sum(means * turned.astype(F32), axis=0, keepdims=True)


def key_kernel(groups, start, added, scale, queries, latents, latents_t, delta, *refs):
    keys, probs, refs = refs[:groups], refs[groups : 2 * groups], refs[2 * groups :]
    before, refs = (refs[:groups], refs[groups:]) if added else (None, refs)
    grads, terms = refs[:groups], refs[groups:]
    key_count, key_width = keys[0].shape
    here = slice(start, start + latents.shape[0])
    for group in range(groups):
        chances = probs[group][:, here]
        grad_probs = dot(keys[group][:, :LATENT], latents_t[...])
        grads[group][...] = (scale * chances.astype(F32) * (grad_probs - delta[...])).astype(BF16)
        term = dot(grads[group][...], queries[here, :])
        term_latent = term[:, :LATENT] + dot(chances, latents[...])
        if not added:
            terms[group][:, :LATENT] = term_latent
            terms[group][:, LATENT:] = term[:, LATENT:]
            continue
        out, place = terms[group % len(terms)], group // len(terms)
        pieces, _, rows, _ = out.shape
        out[:, place, :, :LATENT] = (
            (term_latent + before[group][:, :LATENT]).astype(BF16).reshape(pieces, rows, LATENT)
        )
        out[:, place, :, LATENT:] = (
            (term[:, LATENT:] + before[group][:, LATENT:])
            .astype(BF16)
            .reshape(pieces, rows, key_width - LATENT)
        )


def owner_terms(terms):
    (high, low), rest = wide_levels()
    for level in reversed(rest):
        masks = [0, level[0]] if len(level) == 1 else [0, level[1], level[0], level[0] | level[1]]
        group = len(terms) // len(masks)
        terms = [
            total(
                terms[i], *[across(terms[i + group * j], masks[j]) for j in range(1, len(masks))]
            )
            for i in range(group)
        ]
    return terms[0]


def plane_terms(terms):
    (high, low), _ = wide_levels()
    own, by_low, by_high, corner = terms
    return [own, across(by_low, low), across(by_high, high), across(corner, high | low)]


def query_kernel(groups, heads, index, w_uk, *refs):
    keys_t, refs = refs[:groups], refs[groups:]
    early, late, (grad_nope, grad_pe) = refs[:groups], refs[groups : 2 * groups], refs[2 * groups :]
    tok = grad_nope.shape[0]
    rows = late[0].shape[1] // heads
    ring = tok // rows
    summed = []
    for grads in (early, late):
        part = dot(keys_t[0][...], grads[0][...])
        for group in range(1, groups):
            part = part + dot(keys_t[group][...], grads[group][...])
        summed.append(part.T.astype(BF16))
    summed = jnp.concatenate(summed, axis=0)
    for head in range(heads):
        taken = [summed[(step * heads + head) * rows : (step * heads + head + 1) * rows] for step in range(ring)]
        nope = dot_last(
            jnp.concatenate(taken, axis=0)[:, :LATENT], w_uk[head * NOPE : (head + 1) * NOPE, :]
        ).astype(BF16)
        for step in range(ring):
            place = lax.rem(index[0] + (ring - step), jnp.int32(ring))
            here = pl.ds(pl.multiple_of(place * rows, rows), rows)
            grad_nope[here, head * NOPE : (head + 1) * NOPE] = nope[step * rows : (step + 1) * rows]
            grad_pe[here, head * ROPE : (head + 1) * ROPE] = taken[step][:, LATENT : LATENT + ROPE]


def on_device(
    hidden,
    cotangent,
    routes,
    gates,
    offsets,
    w_gate,
    w_up,
    w_down,
    w_out,
    latent,
    rope_key,
    q_nope,
    q_pe,
    w_uk,
    w_uv,
):
    rows, width = hidden.shape
    tok = q_nope.shape[0]
    heads = q_nope.shape[1] // NOPE
    scale = 1.0 / math.sqrt(NOPE + ROPE)
    wide_size, ring = lax.axis_size("wide"), lax.axis_size("narrow")
    wide_index, ring_index = lax.axis_index("wide"), lax.axis_index("narrow")
    experts = wide_size * ring // 2
    (high, low), rest = wide_levels()
    key_width = LATENT + -(-max(ROPE, 2 * experts) // LANES) * LANES
    shape = jax.ShapeDtypeStruct
    turn = ring_index.astype(jnp.int32).reshape(1)
    (payload,) = call(
        functools.partial(pack_kernel, experts),
        [shape((2, rows, width + key_width - LATENT // 2), BF16)],
        [(turn, SMEM)] + [(value, HBM) for value in (hidden, cotangent, routes.T, gates.T, latent, rope_key.T)],
        0,
        PACK_LIMIT,
        [
            pltpu.VMEM((ROPE, tok), BF16),
            pltpu.VMEM((routes.shape[1], rows), jnp.int32),
            pltpu.VMEM((routes.shape[1], rows), F32),
            pltpu.VMEM((rows, LATENT), BF16),
            pltpu.VMEM((rows, width), BF16),
            pltpu.VMEM((rows, width), BF16),
            pltpu.VMEM((tok, ROPE), BF16),
            pltpu.SemaphoreType.DMA((6,)),
        ],
    )
    payload = payload.reshape(2 * rows, -1)
    order = [0, low, high, high | low]
    for level in rest:
        extra = [0, level[0]] if len(level) == 1 else [0, level[1], level[0], level[0] | level[1]]
        order = [mask ^ more for more in extra for mask in order]
    places = wide_index ^ jnp.array(order, jnp.int32)
    turns = (ring_index - jnp.arange(ring, dtype=jnp.int32)) % ring
    bases = (offsets[places][None, :] * tok + turns[:, None] * rows).reshape(-1, 4)
    query_base = (offsets[wide_index] * tok).reshape(1)
    groups = bases.shape[0]
    columns, key_count = heads * tok, 4 * rows
    work = 2 * key_count * columns * key_width
    row = shape((1, columns), F32)
    routed, keys = routed_sum(payload, rows, w_gate[0].T, w_up[0].T, w_down[0])
    resid_grad = (cotangent.astype(F32) + routed).astype(BF16)
    queries, outs_t, *made = call(
        functools.partial(before_kernel, heads, scale),
        [shape((columns, key_width), BF16), shape((LATENT, columns), F32)]
        + [shape((key_count, columns), BF16)] * groups
        + [shape((key_width, key_count), BF16)] * groups,
        [(turn, SMEM), (bases, SMEM), (query_base, SMEM), q_nope, q_pe, w_uk, *keys],
        2 * work * groups,
        24,
        [
            pltpu.VMEM(q_nope.shape, BF16),
            pltpu.VMEM(q_pe.shape, BF16),
            pltpu.VMEM((key_width, columns), BF16),
            pltpu.VMEM((groups, key_count, columns), F32),
        ],
    )
    probs, keys_t = made[:groups], made[groups:]

    pieces = [resid_grad, along(resid_grad)]
    for step in range(2, ring):
        pieces.append(along(after(pieces[-1], queries) if step == 2 else pieces[-1]))

    def latents_of(start, stop):
        size = (stop - start) * heads * rows
        return call(
            functools.partial(out_kernel, heads, start),
            [shape((size, LATENT), BF16), shape((LATENT, size), BF16), shape((1, size), F32)],
            [w_out, w_uv, outs_t, *pieces[start:stop]],
            work,
            12,
        )

    part = heads * rows
    early = latents_of(0, ring - 1)
    made = call(
        functools.partial(key_kernel, groups, 0, False, scale),
        [shape((key_count, columns - part), BF16)] * groups + [shape((key_count, key_width), F32)] * groups,
        [queries, *early, *keys, *probs],
        3 * work * groups,
        20,
    )
    grads, before = made[:groups], made[groups:]
    late = latents_of(ring - 1, ring)
    count = groups // ring
    late_grads = [None] * groups
    planes = []
    for slabs in (range(1, ring - 1), (ring - 1, 0)):
        chosen = [slab * count + block for slab in slabs for block in range(count)]
        made = call(
            functools.partial(key_kernel, len(chosen), columns - part, True, scale),
            [shape((key_count, part), BF16)] * len(chosen)
            + [shape((4, len(slabs), rows, key_width), BF16)] * count,
            [queries, *late]
            + [values[i] for values in (keys, probs, before) for i in chosen],
            work * len(chosen),
            16,
        )
        for place, group in enumerate(chosen):
            late_grads[group] = made[place]
        sums = owner_terms(made[len(chosen) :])
        planes.append(plane_terms(sums))
    grad_q_nope, grad_q_pe = call(
        functools.partial(query_kernel, groups, heads),
        [shape(q_nope.shape, BF16), shape(q_pe.shape, BF16)],
        [(turn, SMEM), after(w_uk, sums), *keys_t, *grads, *late_grads],
        work * groups,
        16,
    )

    def to_owners(sums, slabs):
        return [
            lax.ppermute(sums[place], "narrow", [(i, (i - slab) % ring) for i in range(ring)])
            for place, slab in enumerate(slabs)
            if slab
        ]

    *first, grad_q_nope, grad_q_pe = lax.optimization_barrier((*planes[0], grad_q_nope, grad_q_pe))
    moving = to_owners(total(*first), range(1, ring - 1))
    done = lax.optimization_barrier((*planes[1], *moving))
    second = total(*done[:4])
    arrived = [second[1], *done[4:], *to_owners(second, (ring - 1, 0))]
    return (
        resid_grad,
        grad_q_nope,
        grad_q_pe,
        sum(part[:, :LATENT].astype(F32) for part in arrived),
        sum(part[:, LATENT : LATENT + ROPE].astype(F32) for part in arrived),
    )


def solution(mesh):
    return jax.shard_map(
        on_device,
        mesh=mesh,
        in_specs=(
            P(("wide", "narrow"), None),
            P(("wide", "narrow"), None),
            P(("wide", "narrow"), None),
            P(("wide", "narrow"), None),
            P(),
            P(("wide", "narrow"), None, None),
            P(("wide", "narrow"), None, None),
            P(("wide", "narrow"), None, None),
            P("narrow", None),
            P("wide", None),
            P("wide", None),
            P("wide", "narrow"),
            P("wide", "narrow"),
            P("narrow", None),
            P("narrow", None),
        ),
        out_specs=(
            P(("wide", "narrow"), None),
            P("wide", "narrow"),
            P("wide", "narrow"),
            P(("wide", "narrow"), None),
            P(("wide", "narrow"), None),
        ),
        check_vma=False,
    )
```

```python
import functools
import math

import jax
import jax.numpy as jnp
from jax import lax
from jax.experimental import pallas as pl
from jax.experimental.pallas import tpu as pltpu
from jax.sharding import PartitionSpec as P

LATENT = 512
NOPE = 128
ROPE = 64
VDIM = 128

F32 = jnp.float32
BF16 = jnp.bfloat16
CONTRACT_LAST = (((1,), (1,)), ((), ()))


def across(value, mask):
    pairs = [(source, source ^ mask) for source in range(lax.axis_size("wide"))]
    return lax.ppermute(value, "wide", pairs)


def along(value):
    size = lax.axis_size("narrow")
    return lax.ppermute(value, "narrow", [(i, (i + 1) % size) for i in range(size)])


def wide_levels():
    size = lax.axis_size("wide")
    masks = []
    mask = size // 2
    while mask:
        masks.append(mask)
        mask //= 2
    first, rest = masks[:2], masks[2:]
    return first, [rest[i : i + 2] for i in range(0, len(rest), 2)]


def gather_level(block, level):
    if len(level) == 1:
        return [block, across(block, level[0])]
    high, low = level
    by_low, by_high = across(block, low), across(block, high)
    half = block.shape[0] // 2
    corner = jnp.concatenate([across(by_low[:half], high), across(by_high[half:], low)], axis=0)
    return [block, by_low, by_high, corner]


def total(*terms):
    summed = terms[0].astype(F32)
    for term in terms[1:]:
        summed = summed + term.astype(F32)
    return summed.astype(BF16)


def scatter_level(blocks, level):
    if len(level) == 1:
        return total(blocks[0], across(blocks[1], level[0]))
    high, low = level
    own, by_low, by_high, corner = blocks
    half = own.shape[1] // 2
    from_high = across(corner[:, :half], high)
    from_low = across(corner[:, half:], low)
    by_low = jnp.concatenate([total(by_low[:, :half], from_high), by_low[:, half:]], axis=1)
    by_high = jnp.concatenate([by_high[:, :half], total(by_high[:, half:], from_low)], axis=1)
    return total(own, across(by_low, low), across(by_high, high))

LANES = 128
PACK_LIMIT = 56
VMEM = pl.BlockSpec(memory_space=pltpu.VMEM)
SMEM = pl.BlockSpec(memory_space=pltpu.SMEM)
HBM = pl.BlockSpec(memory_space=pltpu.HBM)


def dot(left, right):
    return jnp.dot(left, right, preferred_element_type=F32)


def dot_last(left, right):
    return lax.dot_general(left, right, CONTRACT_LAST, preferred_element_type=F32)


def call(kernel, outs, ins, flops, limit, scratch=()):
    specs = [entry[1] if isinstance(entry, tuple) else VMEM for entry in ins]
    arrays = [entry[0] if isinstance(entry, tuple) else entry for entry in ins]
    moved = sum(math.prod(out.shape) * out.dtype.itemsize for out in outs)
    moved += sum(array.size * array.dtype.itemsize for array in arrays)
    return pl.pallas_call(
        kernel,
        out_shape=outs,
        in_specs=specs,
        out_specs=[VMEM] * len(outs),
        scratch_shapes=list(scratch),
        compiler_params=pltpu.CompilerParams(vmem_limit_bytes=limit * 2**20),
        cost_estimate=pl.CostEstimate(flops=flops, bytes_accessed=moved, transcendentals=0),
    )(*arrays)


def pack_kernel(experts, index, hidden, cotangent, routes, gates, latent, rope, out, *scratch):
    *held, turned, sems = scratch
    rows, width = hidden.shape
    half = latent.shape[1] // 2
    tail = out.shape[2] - width - half
    place = pl.ds(pl.multiple_of(index[0] * rows, rows), rows)
    sources = [rope, routes, gates, latent.at[place, :], hidden, cotangent]
    copies = [
        pltpu.make_async_copy(source, target, sems.at[i])
        for i, (source, target) in enumerate(zip(sources, held))
    ]
    for copy in copies:
        copy.start()
    for copy in copies[:3]:
        copy.wait()
    rope_held, routes_held, gates_held, latent_held, hidden_held, cotangent_held = held
    turned[...] = rope_held[...].T
    out[0, :, width + half :] = jnp.zeros((rows, tail), BF16)
    out[0, :, width + half : width + half + ROPE] = turned[place, :]
    line = lax.broadcasted_iota(jnp.int32, (tail, rows), 0)
    first = jnp.zeros((tail, rows), F32)
    second = jnp.zeros((tail, rows), F32)
    for k in range(routes.shape[0]):
        chosen, weight = routes_held[k : k + 1, :], gates_held[k : k + 1, :]
        first = first + jnp.where(line == chosen, weight, 0.0)
        second = second + jnp.where(line == chosen + experts, weight, 0.0)
    second = second - second.astype(BF16).astype(F32)
    out[1, :, width + half :] = (first + second).T.astype(BF16)
    for copy in copies[3:]:
        copy.wait()
    out[0, :, width : width + half] = latent_held[:, :half]
    out[1, :, width : width + half] = latent_held[:, half:]
    out[0, :, :width] = hidden_held[...]
    out[1, :, :width] = cotangent_held[...]


def expert_kernel(experts, expert_ref, tokens, w_gate, w_up, w_down, keys, out):
    pieces, _, rows, wide = tokens.shape
    width = w_down.shape[1]
    merged = pieces * rows
    tail = keys.shape[1] - LATENT
    half = wide - tail
    x_rows = tokens[:, 0, :, :width].reshape(merged, width)
    dy_rows = tokens[:, 1, :, :width].reshape(merged, width)
    keys[:, : half - width] = tokens[:, 0, :, width:half].reshape(merged, half - width)
    keys[:, half - width : LATENT] = tokens[:, 1, :, width:half].reshape(merged, half - width)
    keys[:, LATENT:] = tokens[:, 0, :, half:].reshape(merged, tail)
    parts = tokens[:, 1, :, half:].reshape(merged, tail).astype(F32)
    lane = lax.broadcasted_iota(jnp.int32, (merged, tail), 1)
    mine = (lane == expert_ref[0]) | (lane == expert_ref[0] + experts)
    gate = jnp.sum(jnp.where(mine, parts, 0.0), axis=1, keepdims=True)
    pre_gate = dot_last(x_rows, w_gate[...])
    up_value = dot_last(x_rows, w_up[...])
    grad_hidden = gate * dot_last(dy_rows, w_down[...])
    sigmoid_gate = jax.nn.sigmoid(pre_gate)
    scaled = grad_hidden * sigmoid_gate
    grad_gate = scaled * up_value * (1.0 + pre_gate * (1.0 - sigmoid_gate))
    grad_up = scaled * pre_gate
    partial_grad = dot(grad_gate.astype(BF16), w_gate[...]) + dot(grad_up.astype(BF16), w_up[...])
    out[...] = partial_grad.astype(BF16)


def after(value, *earlier):
    return lax.optimization_barrier((value, *earlier))[0]


def routed_sum(payload, rows, w_gate, w_up, w_down):
    wide_size, ring = lax.axis_size("wide"), lax.axis_size("narrow")
    wide_index, ring_index = lax.axis_index("wide"), lax.axis_index("narrow")
    experts = wide_size * ring // 2
    expert = ((wide_index * ring + ring_index) // 2).astype(jnp.int32).reshape(1)
    wide, width = payload.shape[1], w_down.shape[1]
    (high, low), rest = wide_levels()
    key_width = LATENT + wide - width - LATENT // 2

    def experts_of(block):
        return call(
            functools.partial(expert_kernel, experts),
            [jax.ShapeDtypeStruct((4 * rows, key_width), BF16), jax.ShapeDtypeStruct((4 * rows, width), BF16)],
            [(expert, SMEM), block.reshape(4, 2, rows, wide), w_gate, w_up, w_down],
            40 * rows * w_down.size,
            14,
        )

    def spread(block):
        blocks = [block]
        for level in rest:
            blocks = [piece for one in zip(*[gather_level(b, level) for b in blocks]) for piece in one]
        return blocks

    def collect(sums):
        if len(sums) == 2:
            moved = across(sums[1], rest[0][0])
            return [
                total(sums[0][i * rows : (i + 1) * rows], moved[i * rows : (i + 1) * rows]) for i in range(4)
            ]
        for level in reversed(rest):
            group = len(sums) // 2 ** len(level)
            sums = [
                scatter_level([sums[i + group * j] for j in range(2 ** len(level))], level)
                for i in range(group)
            ]
        return list(sums[0].reshape(4, rows, width))

    def together(*values):
        return list(lax.optimization_barrier(values))

    def with_room(column):
        return jnp.concatenate([column, column[:rows]], axis=0)

    def filled(room, half):
        return lax.dynamic_update_slice_in_dim(room, half, 2 * rows, 0)

    slabs, results, sums = [], [], []
    column, rooms, sides, former = payload, None, None, None
    for turn in range(ring + 1):
        if turn == 0:
            moving = [across(column, low), across(column, high), along(column)]
            beside = []
        else:
            halves = [sides[1][rows:], sides[0][:rows]]
            sent = [filled(*pair) for pair in zip(rooms, halves)] if turn < ring else halves
            moving = [across(sent[0], low), across(sent[1], high)]
            if turn < ring - 1:
                moving.append(along(column))
            beside = []
        if turn > 1:
            blocks = spread(after(slabs[turn - 2], *sent))
            results.append([experts_of(block) for block in blocks])
            beside += [result[1] for result in results[-1]][: None if turn < ring else 1]
        if turn > 2:
            sums.append(collect([result[1] for result in results[turn - 3]]))
            beside += sums[-1]
        if turn < ring - 1:
            beside += [with_room(moving[2]), with_room(moving[2])]
        done = together(*moving, *beside)
        if turn > 0:
            corner = [part[-rows:] for part in done[:2]]
            slabs.append(jnp.concatenate([former, *sides, corner[1], corner[0]], axis=0))
        if turn < ring:
            sides = [part[: 2 * rows] for part in done[:2]]
        former = column
        if turn < ring - 1:
            column, rooms = done[2], done[-2:]

    def parts_of(step):
        return sums[step]

    last = ring - 1
    link = corner = None
    for step in range(1, last - 1):
        own, by_low, by_high, far = parts_of(step)
        moving = [
            across(by_low, low),
            across(by_high, high),
            along(far if corner is None else total(far, corner)),
        ]
        if link is not None:
            moving.append(along(link))
        count, beside = len(moving), []
        if step == last - 2:
            first, *others = spread(slabs[last])
            before = [result[1] for result in results[last - 1]]
            beside = [*before[1:], *others]
        done = together(*moving, *beside)
        corner = done[2]
        link = total(own, *done[:2], *done[3:count])
    others = [experts_of(block) for block in done[-len(others) :]]
    sums.append(collect(before))
    home, home_low, home_high, home_far = parts_of(0)
    link, home_far, *done = together(
        along(link), across(home_far, high | low), *sums[last - 1], *[result[1] for result in others]
    )
    sums[last - 1] = done[:4]
    own, by_low, by_high, far = parts_of(last - 1)
    first = experts_of(after(first, home_far))
    results.append([first, *others])
    sums.append(collect([result[1] for result in results[last]]))
    by_low, by_high, corner, *sums[last] = together(
        across(by_low, low), across(by_high, high), along(total(far, corner)), *sums[last]
    )
    link = total(own, by_low, by_high, link)
    own, by_low, by_high, far = parts_of(last)
    done = together(
        across(by_low, low),
        across(by_high, high),
        across(total(far, corner), high | low),
        along(link),
    )
    link = total(own, *done)
    home_low, home_high, link = together(home_low, home_high, link)
    done = together(along(link), across(home_low, low), across(home_high, high))
    summed = sum(part.astype(F32) for part in (home, home_far, *done))
    return summed, [result[0] for slab in results for result in slab]


def before_kernel(heads, scale, index, bases, query_base, q_nope, q_pe, w_uk, *refs):
    groups, pieces = bases.shape
    keys, (queries, outs_t, *rest), (nope, pe, queries_t, scores) = refs[:groups], refs[groups:-4], refs[-4:]
    probs, keys_t = rest[:groups], rest[groups:]
    tok = q_nope.shape[0]
    key_count, key_width = keys[0].shape
    columns = heads * tok
    rows = key_count // pieces
    ring = tok // rows
    for step in range(ring):
        place = lax.rem(index[0] + (ring - step), jnp.int32(ring))
        source, target = pl.ds(pl.multiple_of(place * rows, rows), rows), pl.ds(step * rows, rows)
        nope[target, :] = q_nope[source, :]
        pe[target, :] = q_pe[source, :]
    queries[:, LATENT:] = jnp.zeros((columns, key_width - LATENT), BF16)
    for head in range(heads):
        made = dot(
            nope[:, head * NOPE : (head + 1) * NOPE], w_uk[head * NOPE : (head + 1) * NOPE, :]
        ).astype(BF16)
        for step in range(ring):
            here = pl.ds((step * heads + head) * rows, rows)
            part = slice(step * rows, (step + 1) * rows)
            queries[here, :LATENT] = made[part]
            queries[here, LATENT : LATENT + ROPE] = pe[part, head * ROPE : (head + 1) * ROPE]
    queries_t[...] = queries[...].T
    column = lax.broadcasted_iota(jnp.int32, (1, columns), 1)
    place = lax.rem(index[0] + (ring - lax.div(column, jnp.int32(heads * rows))), jnp.int32(ring))
    position = query_base[0] + place * rows + lax.rem(column, jnp.int32(rows))
    ahead = lax.broadcasted_iota(jnp.int32, (rows, columns), 0) - position
    highest = jnp.full((1, columns), -1e30, F32)
    for group in range(groups):
        raw = dot(keys[group][...], queries_t[...])
        for piece in range(pieces):
            here = slice(piece * rows, (piece + 1) * rows)
            shown = ahead + bases[group, piece] <= 0
            masked = jnp.where(shown, raw[here, :] * scale, -1e30)
            scores[group, here, :] = masked
            highest = jnp.maximum(highest, jnp.max(masked, axis=0, keepdims=True))
        keys_t[group][...] = keys[group][...].T
    norm = jnp.zeros((1, columns), F32)
    for group in range(groups):
        grown = jnp.exp(scores[group] - highest)
        scores[group] = grown
        norm = norm + jnp.sum(grown, axis=0, keepdims=True)
    inverse = 1.0 / norm
    for group in range(groups):
        probs[group][...] = (scores[group] * inverse).astype(BF16)
        part = dot(keys_t[group][:LATENT, :], probs[group][...])
        if group == 0:
            outs_t[...] = part
        else:
            outs_t[...] += part


def out_kernel(heads, start, w_out, w_uv, outs_t, *refs):
    resid, (latents, latents_t, delta) = refs[:-3], refs[-3:]
    rows = resid[0].shape[0]
    moved = jnp.concatenate([part[...] for part in resid], axis=0)
    grad_out = dot_last(moved, w_out[...]).astype(BF16)
    for head in range(heads):
        made = dot(
            grad_out[:, head * VDIM : (head + 1) * VDIM], w_uv[head * VDIM : (head + 1) * VDIM, :]
        ).astype(BF16)
        for step in range(len(resid)):
            latents[pl.ds((step * heads + head) * rows, rows), :] = made[step * rows : (step + 1) * rows]
    turned = latents[...].T
    latents_t[...] = turned
    first = start * heads * rows
    means = outs_t[:, first : first + turned.shape[1]]
    delta[...] = jnp.sum(means * turned.astype(F32), axis=0, keepdims=True)


def key_kernel(groups, start, added, scale, queries, latents, latents_t, delta, *refs):
    keys, probs, refs = refs[:groups], refs[groups : 2 * groups], refs[2 * groups :]
    before, refs = (refs[:groups], refs[groups:]) if added else (None, refs)
    grads, terms = refs[:groups], refs[groups:]
    key_count, key_width = keys[0].shape
    here = slice(start, start + latents.shape[0])
    for group in range(groups):
        chances = probs[group][:, here]
        grad_probs = dot(keys[group][:, :LATENT], latents_t[...])
        grads[group][...] = (scale * chances.astype(F32) * (grad_probs - delta[...])).astype(BF16)
        term = dot(grads[group][...], queries[here, :])
        term_latent = term[:, :LATENT] + dot(chances, latents[...])
        if not added:
            terms[group][:, :LATENT] = term_latent
            terms[group][:, LATENT:] = term[:, LATENT:]
            continue
        out, place = terms[group % len(terms)], group // len(terms)
        pieces, _, rows, _ = out.shape
        out[:, place, :, :LATENT] = (
            (term_latent + before[group][:, :LATENT]).astype(BF16).reshape(pieces, rows, LATENT)
        )
        out[:, place, :, LATENT:] = (
            (term[:, LATENT:] + before[group][:, LATENT:])
            .astype(BF16)
            .reshape(pieces, rows, key_width - LATENT)
        )


def owner_terms(terms):
    (high, low), rest = wide_levels()
    for level in reversed(rest):
        masks = [0, level[0]] if len(level) == 1 else [0, level[1], level[0], level[0] | level[1]]
        group = len(terms) // len(masks)
        terms = [
            total(
                terms[i], *[across(terms[i + group * j], masks[j]) for j in range(1, len(masks))]
            )
            for i in range(group)
        ]
    return terms[0]


def plane_terms(terms):
    (high, low), _ = wide_levels()
    own, by_low, by_high, corner = terms
    return [own, across(by_low, low), across(by_high, high), across(corner, high | low)]


def query_kernel(groups, heads, index, w_uk, *refs):
    keys_t, refs = refs[:groups], refs[groups:]
    early, late, (grad_nope, grad_pe) = refs[:groups], refs[groups : 2 * groups], refs[2 * groups :]
    tok = grad_nope.shape[0]
    rows = late[0].shape[1] // heads
    ring = tok // rows
    summed = []
    for grads in (early, late):
        part = dot(keys_t[0][...], grads[0][...])
        for group in range(1, groups):
            part = part + dot(keys_t[group][...], grads[group][...])
        summed.append(part.T.astype(BF16))
    summed = jnp.concatenate(summed, axis=0)
    for head in range(heads):
        taken = [summed[(step * heads + head) * rows : (step * heads + head + 1) * rows] for step in range(ring)]
        nope = dot_last(
            jnp.concatenate(taken, axis=0)[:, :LATENT], w_uk[head * NOPE : (head + 1) * NOPE, :]
        ).astype(BF16)
        for step in range(ring):
            place = lax.rem(index[0] + (ring - step), jnp.int32(ring))
            here = pl.ds(pl.multiple_of(place * rows, rows), rows)
            grad_nope[here, head * NOPE : (head + 1) * NOPE] = nope[step * rows : (step + 1) * rows]
            grad_pe[here, head * ROPE : (head + 1) * ROPE] = taken[step][:, LATENT : LATENT + ROPE]


def on_device(
    hidden,
    cotangent,
    routes,
    gates,
    offsets,
    w_gate,
    w_up,
    w_down,
    w_out,
    latent,
    rope_key,
    q_nope,
    q_pe,
    w_uk,
    w_uv,
):
    rows, width = hidden.shape
    tok = q_nope.shape[0]
    heads = q_nope.shape[1] // NOPE
    scale = 1.0 / math.sqrt(NOPE + ROPE)
    wide_size, ring = lax.axis_size("wide"), lax.axis_size("narrow")
    wide_index, ring_index = lax.axis_index("wide"), lax.axis_index("narrow")
    experts = wide_size * ring // 2
    (high, low), rest = wide_levels()
    key_width = LATENT + -(-max(ROPE, 2 * experts) // LANES) * LANES
    shape = jax.ShapeDtypeStruct
    turn = ring_index.astype(jnp.int32).reshape(1)
    (payload,) = call(
        functools.partial(pack_kernel, experts),
        [shape((2, rows, width + key_width - LATENT // 2), BF16)],
        [(turn, SMEM)] + [(value, HBM) for value in (hidden, cotangent, routes.T, gates.T, latent, rope_key.T)],
        0,
        PACK_LIMIT,
        [
            pltpu.VMEM((ROPE, tok), BF16),
            pltpu.VMEM((routes.shape[1], rows), jnp.int32),
            pltpu.VMEM((routes.shape[1], rows), F32),
            pltpu.VMEM((rows, LATENT), BF16),
            pltpu.VMEM((rows, width), BF16),
            pltpu.VMEM((rows, width), BF16),
            pltpu.VMEM((tok, ROPE), BF16),
            pltpu.SemaphoreType.DMA((6,)),
        ],
    )
    payload = payload.reshape(2 * rows, -1)
    order = [0, low, high, high | low]
    for level in rest:
        extra = [0, level[0]] if len(level) == 1 else [0, level[1], level[0], level[0] | level[1]]
        order = [mask ^ more for more in extra for mask in order]
    places = wide_index ^ jnp.array(order, jnp.int32)
    turns = (ring_index - jnp.arange(ring, dtype=jnp.int32)) % ring
    bases = (offsets[places][None, :] * tok + turns[:, None] * rows).reshape(-1, 4)
    query_base = (offsets[wide_index] * tok).reshape(1)
    groups = bases.shape[0]
    columns, key_count = heads * tok, 4 * rows
    work = 2 * key_count * columns * key_width
    row = shape((1, columns), F32)
    routed, keys = routed_sum(payload, rows, w_gate[0].T, w_up[0].T, w_down[0])
    resid_grad = (cotangent.astype(F32) + routed).astype(BF16)
    queries, outs_t, *made = call(
        functools.partial(before_kernel, heads, scale),
        [shape((columns, key_width), BF16), shape((LATENT, columns), F32)]
        + [shape((key_count, columns), BF16)] * groups
        + [shape((key_width, key_count), BF16)] * groups,
        [(turn, SMEM), (bases, SMEM), (query_base, SMEM), q_nope, q_pe, w_uk, *keys],
        2 * work * groups,
        24,
        [
            pltpu.VMEM(q_nope.shape, BF16),
            pltpu.VMEM(q_pe.shape, BF16),
            pltpu.VMEM((key_width, columns), BF16),
            pltpu.VMEM((groups, key_count, columns), F32),
        ],
    )
    probs, keys_t = made[:groups], made[groups:]

    pieces = [resid_grad, along(resid_grad)]
    for step in range(2, ring):
        pieces.append(along(after(pieces[-1], queries) if step == 2 else pieces[-1]))

    def latents_of(start, stop):
        size = (stop - start) * heads * rows
        return call(
            functools.partial(out_kernel, heads, start),
            [shape((size, LATENT), BF16), shape((LATENT, size), BF16), shape((1, size), F32)],
            [w_out, w_uv, outs_t, *pieces[start:stop]],
            work,
            12,
        )

    part = heads * rows
    early = latents_of(0, ring - 1)
    made = call(
        functools.partial(key_kernel, groups, 0, False, scale),
        [shape((key_count, columns - part), BF16)] * groups + [shape((key_count, key_width), F32)] * groups,
        [queries, *early, *keys, *probs],
        3 * work * groups,
        20,
    )
    grads, before = made[:groups], made[groups:]
    late = latents_of(ring - 1, ring)
    count = groups // ring
    late_grads = [None] * groups
    planes = []
    for slabs in (range(1, ring - 1), (ring - 1, 0)):
        chosen = [slab * count + block for slab in slabs for block in range(count)]
        made = call(
            functools.partial(key_kernel, len(chosen), columns - part, True, scale),
            [shape((key_count, part), BF16)] * len(chosen)
            + [shape((4, len(slabs), rows, key_width), BF16)] * count,
            [queries, *late]
            + [values[i] for values in (keys, probs, before) for i in chosen],
            work * len(chosen),
            16,
        )
        for place, group in enumerate(chosen):
            late_grads[group] = made[place]
        sums = owner_terms(made[len(chosen) :])
        planes.append(plane_terms(sums))
    grad_q_nope, grad_q_pe = call(
        functools.partial(query_kernel, groups, heads),
        [shape(q_nope.shape, BF16), shape(q_pe.shape, BF16)],
        [(turn, SMEM), after(w_uk, sums), *keys_t, *grads, *late_grads],
        work * groups,
        16,
    )

    def to_owners(sums, slabs):
        return [
            lax.ppermute(sums[place], "narrow", [(i, (i - slab) % ring) for i in range(ring)])
            for place, slab in enumerate(slabs)
            if slab
        ]

    *first, grad_q_nope, grad_q_pe = lax.optimization_barrier((*planes[0], grad_q_nope, grad_q_pe))
    moving = to_owners(total(*first), range(1, ring - 1))
    done = lax.optimization_barrier((*planes[1], *moving))
    second = total(*done[:4])
    arrived = [second[1], *done[4:], *to_owners(second, (ring - 1, 0))]
    return (
        resid_grad,
        grad_q_nope,
        grad_q_pe,
        sum(part[:, :LATENT].astype(F32) for part in arrived),
        sum(part[:, LATENT : LATENT + ROPE].astype(F32) for part in arrived),
    )


def solution(mesh):
    return jax.shard_map(
        on_device,
        mesh=mesh,
        in_specs=(
            P(("wide", "narrow"), None),
            P(("wide", "narrow"), None),
            P(("wide", "narrow"), None),
            P(("wide", "narrow"), None),
            P(),
            P(("wide", "narrow"), None, None),
            P(("wide", "narrow"), None, None),
            P(("wide", "narrow"), None, None),
            P("narrow", None),
            P("wide", None),
            P("wide", None),
            P("wide", "narrow"),
            P("wide", "narrow"),
            P("narrow", None),
            P("narrow", None),
        ),
        out_specs=(
            P(("wide", "narrow"), None),
            P("wide", "narrow"),
            P("wide", "narrow"),
            P(("wide", "narrow"), None),
            P(("wide", "narrow"), None),
        ),
        check_vma=False,
    )
```
